128 devices in a mesh: energy: 16 (over z, y_lo, core), momentum: 8 (over y_hi, x).
Axes of the slice: x: 4, y: 4 (y_hi: 2, y_lo: 2; y = y_hi * 2 + y_lo), z: 4, core: 2. Of those that a mesh axis runs over, the one named last changes fastest.
Arguments:
- green_ret: bfloat16 [32, 16, 2, 512, 512], P('energy', 'momentum'), may hold values from -0.1875 to 0.1875
- sigma_in: bfloat16 [32, 16, 2, 512, 512], P('energy', 'momentum'), may hold values from -6 to 6
- screened: bfloat16 [128, 32, 16, 2, 2048], P(('energy', 'momentum')), may hold values from -6 to 6
- block_of_slot: int32 [128], replicated, may hold values from 0 to 127, each once
Outputs:
- green_new: bfloat16 [32, 16, 2, 512, 512], P('energy', 'momentum')
The draws below stay inside these ranges and needn't reach their ends.
Inputs may be any that keep to these rules, and one draw needn't show every extreme that they name: block_of_slot is a permutation of the blocks 0 to 127.
All inputs are finite; a program needn't handle non-finite values.
Results may differ from the reference program's by a relative error of at most 0.0085.
Values may be sent and summed in bfloat16 or wider, within the bound.
A program may use at most 128 MiB of HBM per device.

```python
import jax
import jax.numpy as jnp
from jax import lax

NO = 512
NE = 32
NK = 16
NBLK = 128
PB = 2048


def shard_levels(own_key, shape, cuts, least, top_value):
    gain, own = 1.0, jax.random.fold_in(own_key, 6)
    for axis_at, parts in cuts:
        steps = jnp.exp(jax.random.uniform(jax.random.fold_in(own, axis_at), (parts,), jnp.float32, least / len(cuts), top_value / len(cuts)))
        gain = gain * jnp.repeat(steps, shape[axis_at] // parts).reshape([-1 if axis == axis_at else 1 for axis in range(len(shape))])
    return gain


def normal_values(rng, shape, width, most, shards=(), dtype=jnp.bfloat16):
    values = width * jax.random.normal(rng, shape, jnp.float32)
    if shards:
        values = values * shard_levels(rng, shape, shards, -0.22, 0.18)
    return jnp.clip(values, -most, most).astype(dtype)


def setup_inputs(seed: int = 0) -> dict:
    streams_of = jax.random.split(jax.random.key(seed), 5)
    green_ret = normal_values(streams_of[0], (NE, NK, 2, NO, NO), (2 * NO) ** -0.5, 0.1875, ((0, 16), (1, 8)))
    sigma_in = normal_values(streams_of[1], (NE, NK, 2, NO, NO), 1.0, 6.0, ((0, 16), (1, 8)))
    screened = normal_values(streams_of[2], (NBLK, NE, NK, 2, PB), 0.7, 6.0, ((0, 128),))
    block_of_slot = jax.random.permutation(streams_of[3], NBLK).astype(jnp.int32)
    return {"green_ret": green_ret, "sigma_in": sigma_in, "screened": screened, "block_of_slot": block_of_slot}


def matmul(left_side, right_side):
    return jnp.dot(left_side, right_side, preferred_element_type=jnp.float32)


def sandwich(green, sigma):
    green_real = green[0]
    green_imag = green[1]
    sigma_real = sigma[0]
    sigma_imag = sigma[1]
    first_real = (matmul(green_real, sigma_real) - matmul(green_imag, sigma_imag)).astype(jnp.bfloat16)
    first_imag = (matmul(green_real, sigma_imag) + matmul(green_imag, sigma_real)).astype(jnp.bfloat16)
    second_real = matmul(first_real, green_real.T) + matmul(first_imag, green_imag.T)
    second_imag = matmul(first_imag, green_real.T) - matmul(first_real, green_imag.T)
    return jnp.stack([second_real, second_imag]).astype(jnp.bfloat16)


def sandwich_all(green, sigma):
    flat_green = green.reshape(NE * NK, 2, NO, NO)
    flat_sigma = sigma.reshape(NE * NK, 2, NO, NO)
    result = lax.map(lambda both: sandwich(both[0], both[1]), (flat_green, flat_sigma))
    return result.reshape(NE, NK, 2, NO, NO)


def reference(green_ret, sigma_in, screened, block_of_slot):
    green = sandwich_all(green_ret, sigma_in)
    blocks = green.reshape(NE, NK, 2, NBLK, PB)

    def convolve_slot(both):
        block_index, weight = both
        piece = lax.dynamic_index_in_dim(blocks, block_index, axis=3, keepdims=False).astype(jnp.float32)
        values = lax.complex(piece[:, :, 0], piece[:, :, 1])
        spectrum = jnp.fft.fft2(values, axes=(0, 1))
        factor = lax.complex(weight[:, :, 0].astype(jnp.float32), weight[:, :, 1].astype(jnp.float32))
        result = jnp.fft.ifft2(spectrum * factor, axes=(0, 1))
        return jnp.stack([jnp.real(result), jnp.imag(result)], axis=2).astype(jnp.bfloat16)

    convolved = lax.map(convolve_slot, (block_of_slot, screened))
    restored = jnp.zeros_like(blocks).at[:, :, :, block_of_slot, :].set(jnp.moveaxis(convolved, 0, 3))
    sigma_new = restored.reshape(NE, NK, 2, NO, NO)
    return sandwich_all(green_ret, sigma_new)
```

```python
import functools

import jax
import jax.numpy as jnp
from jax import lax
from jax.experimental import pallas as pl
from jax.experimental.pallas import tpu as pltpu
from jax.sharding import PartitionSpec as P


def plain_product(left_side, right_side):
    return jnp.einsum("abij,abjl->abil", left_side, right_side, preferred_element_type=jnp.float32)


def adjoint_product(left_side, right_side):
    return jnp.einsum("abij,ablj->abil", left_side, right_side, preferred_element_type=jnp.float32)


def sandwich(green, sigma):
    green_real = green[:, :, 0]
    green_imag = green[:, :, 1]
    sigma_real = sigma[:, :, 0]
    sigma_imag = sigma[:, :, 1]
    first_real = (
        plain_product(green_real, sigma_real) - plain_product(green_imag, sigma_imag)
    ).astype(jnp.bfloat16)
    first_imag = (
        plain_product(green_real, sigma_imag) + plain_product(green_imag, sigma_real)
    ).astype(jnp.bfloat16)
    second_real = adjoint_product(first_real, green_real) + adjoint_product(first_imag, green_imag)
    second_imag = adjoint_product(first_imag, green_real) - adjoint_product(first_real, green_imag)
    return jnp.stack([second_real, second_imag], axis=2).astype(jnp.bfloat16)


def tables(length):
    counter = jnp.arange(length, dtype=jnp.int32)
    phases = counter[:, None] * counter[None, :] % length
    angles = phases.astype(jnp.float32) * (2.0 * jnp.pi / length)
    return (jnp.cos(angles), jnp.sin(angles))


def along_energy(table, values):
    return jnp.einsum("me,ekp->mkp", table, values, precision=lax.Precision.HIGH)


def along_momentum(table, values):
    return jnp.einsum("nk,mkp->mnp", table, values, precision=lax.Precision.HIGH)


def convolve(gathered, weight):
    energies = gathered.shape[0]
    momenta = gathered.shape[1]
    cos_energy, sin_energy = tables(energies)
    cos_momentum, sin_momentum = tables(momenta)
    values = gathered.astype(jnp.float32)
    value_real = values[:, :, 0]
    value_imag = values[:, :, 1]
    half_real = along_energy(cos_energy, value_real) + along_energy(sin_energy, value_imag)
    half_imag = along_energy(cos_energy, value_imag) - along_energy(sin_energy, value_real)
    spec_real = along_momentum(cos_momentum, half_real) + along_momentum(sin_momentum, half_imag)
    spec_imag = along_momentum(cos_momentum, half_imag) - along_momentum(sin_momentum, half_real)
    weight_real = weight[:, :, 0].astype(jnp.float32)
    weight_imag = weight[:, :, 1].astype(jnp.float32)
    times_real = spec_real * weight_real - spec_imag * weight_imag
    times_imag = spec_real * weight_imag + spec_imag * weight_real
    back_real = along_momentum(cos_momentum, times_real) - along_momentum(sin_momentum, times_imag)
    back_imag = along_momentum(cos_momentum, times_imag) + along_momentum(sin_momentum, times_real)
    final_real = along_energy(cos_energy, back_real) - along_energy(sin_energy, back_imag)
    final_imag = along_energy(cos_energy, back_imag) + along_energy(sin_energy, back_real)
    factor = 1.0 / (energies * momenta)
    return (jnp.stack([final_real, final_imag], axis=2) * factor).astype(jnp.bfloat16)


def exchange_kernel(src, dst, send_sem, recv_sem, own_sem):
    e = lax.axis_index("energy")
    m = lax.axis_index("momentum")
    me = e * 8 + m

    def partner(i):
        core, z, y, x = i % 2, (i // 2) % 4, (i // 8) % 4, i // 32
        my_y = (m // 4) * 2 + (e // 2) % 2
        to_x = (m % 4 + x) % 4
        to_y = (my_y + y) % 4
        to_z = (e // 4 + z) % 4
        to_core = (e % 2 + core) % 2
        return to_z * 4 + (to_y % 2) * 2 + to_core, (to_y // 2) * 4 + to_x

    barrier = pltpu.get_barrier_semaphore()

    def greet(i, _):
        pl.semaphore_signal(barrier, inc=1, device_id=partner(i), device_id_type=pl.DeviceIdType.MESH)
        return 0

    lax.fori_loop(1, 128, greet, 0)
    pl.semaphore_wait(barrier, 127)
    for chunk in range(4):
        def send(i, _):
            to = partner(i)
            pltpu.make_async_remote_copy(
                src.at[chunk, to[0] * 8 + to[1]],
                dst.at[chunk, me],
                send_sem.at[chunk],
                recv_sem.at[chunk],
                device_id=to,
                device_id_type=pl.DeviceIdType.MESH,
            ).start()
            return 0

        lax.fori_loop(1, 128, send, 0)
        pltpu.make_async_copy(src.at[chunk, me], dst.at[chunk, me], own_sem.at[chunk]).start()
    for chunk in range(4):
        pltpu.make_async_copy(src.at[chunk, me], dst.at[chunk, me], own_sem.at[chunk]).wait()
        some = pl.ds(0, 127)
        pltpu.make_async_copy(src.at[chunk, some], dst.at[chunk, some], recv_sem.at[chunk]).wait()
        pltpu.make_async_copy(src.at[chunk, some], dst.at[chunk, some], send_sem.at[chunk]).wait()


def exchange(values):
    return pl.pallas_call(
        exchange_kernel,
        out_shape=jax.ShapeDtypeStruct(values.shape, values.dtype),
        in_specs=[pl.BlockSpec(memory_space=pltpu.VMEM)],
        out_specs=pl.BlockSpec(memory_space=pltpu.VMEM),
        scratch_shapes=[pltpu.SemaphoreType.DMA((4,))] * 3,
        compiler_params=pltpu.CompilerParams(
            collective_id=0, has_side_effects=True, vmem_limit_bytes=20 << 20
        ),
    )(values)


def reorder_kernel(inverse, order, src, dst):
    def move(slot, _):
        block = order[slot]
        if inverse:
            dst[:, block] = src[:, slot]
        else:
            dst[:, slot] = src[:, block]
        return 0

    lax.fori_loop(0, 128, move, 0)


def reorder(values, order, inverse):
    return pl.pallas_call(
        functools.partial(reorder_kernel, inverse),
        out_shape=jax.ShapeDtypeStruct(values.shape, values.dtype),
        in_specs=[
            pl.BlockSpec(memory_space=pltpu.SMEM),
            pl.BlockSpec(memory_space=pltpu.VMEM),
        ],
        out_specs=pl.BlockSpec(memory_space=pltpu.VMEM),
        compiler_params=pltpu.CompilerParams(vmem_limit_bytes=20 << 20),
    )(order, values)


def local(green_ret, sigma_in, screened, block_of_slot):
    green = sandwich(green_ret, sigma_in)
    blocks = green.reshape(2, 2, 2, 128, 2048).transpose(0, 1, 3, 2, 4).reshape(4, 128, 32, 128)
    outgoing = reorder(blocks, block_of_slot, False)
    arrived = exchange(outgoing).reshape(2, 2, 16, 8, 2, 2048)
    gathered = arrived.transpose(2, 0, 3, 1, 4, 5).reshape(32, 16, 2, 2048)
    sigma_slot = convolve(gathered, screened[0])
    back = sigma_slot.reshape(16, 2, 8, 2, 2, 2048).transpose(1, 3, 0, 2, 4, 5).reshape(4, 128, 32, 128)
    restored = reorder(exchange(back), block_of_slot, True).reshape(2, 2, 128, 2, 2048)
    sigma_new = restored.transpose(0, 1, 3, 2, 4).reshape(2, 2, 2, 512, 512)
    return sandwich(green_ret, sigma_new)


def solution(mesh):
    in_specs = (
        P("energy", "momentum", None, None, None),
        P("energy", "momentum", None, None, None),
        P(("energy", "momentum"), None, None, None, None),
        P(),
    )
    out_specs = P("energy", "momentum", None, None, None)
    return jax.shard_map(local, mesh=mesh, in_specs=in_specs, out_specs=out_specs, check_vma=False)
```

```python
import jax
import jax.numpy as jnp
import numpy as np
from jax import lax
from jax.experimental import pallas as pl
from jax.experimental.pallas import tpu as pltpu
from jax.sharding import PartitionSpec as P

BF = jnp.bfloat16
F32 = jnp.float32
CHUNKS = 4
WIDE = 128


def transforms():
    m, n = np.arange(16), np.arange(8)
    e, k = np.arange(16), np.arange(8)
    out = np.zeros((4, 256, 256), np.float64)
    for a in range(2):
        for b in range(2):
            steps = ((2 * m + a)[:, None, None, None] * e[None, None, :, None]) * 1.0 / 32
            steps = steps + ((2 * n + b)[None, :, None, None] * k[None, None, None, :]) * 1.0 / 16
            cos, sin = np.cos(2 * np.pi * steps), np.sin(2 * np.pi * steps)
            cols = np.zeros((2, 16, 8, 16, 8, 2))
            cols[0, ..., 0], cols[0, ..., 1] = cos, sin
            cols[1, ..., 0], cols[1, ..., 1] = -sin, cos
            cols = cols.reshape(2, 16, 8, 8, 2, 4, 2, 2).transpose(0, 1, 2, 3, 5, 4, 6, 7)
            out[2 * a + b] = cols.reshape(256, 256)
    back = out.transpose(0, 2, 1) / 512
    return jnp.asarray(out, BF), jnp.asarray(back, BF)


def swapper():
    row = np.arange(256)
    swapped = (row % 8) * 32 + (row // 8 % 4) * 8 + row // 32
    return jnp.asarray(np.arange(256)[None, :] == swapped[:, None], BF)


def dot(a, b):
    return jnp.dot(a, b, preferred_element_type=F32)


def dot_t(a, b):
    return lax.dot_general(a, b, (((1,), (1,)), ((), ())), preferred_element_type=F32)


def kernel(
    order, green, sigma, weight, forth, back, swap, out,
    g, s, w, tf, ti, sw, rows, cols, first, gbuf, gcol, stage1, got1, stage2, got2, sig, acc,
    load_sem, send1, recv1, send2, recv2, out_sem,
):
    e = lax.axis_index("energy")
    m = lax.axis_index("momentum")
    me = e * 8 + m

    def partner(i):
        core, z, y, x = i % 2, (i // 2) % 4, (i // 8) % 4, i // 32
        my_y = (m // 4) * 2 + (e // 2) % 2
        to_x = (m % 4 + x) % 4
        to_y = (my_y + y) % 4
        to_z = (e // 4 + z) % 4
        to_core = (e % 2 + core) % 2
        return to_z * 4 + (to_y % 2) * 2 + to_core, (to_y // 2) * 4 + to_x

    def load_point(pt):
        return (
            pltpu.make_async_copy(green.at[pt], g.at[pt], load_sem.at[pt]),
            pltpu.make_async_copy(sigma.at[pt], s.at[pt], load_sem.at[4 + pt]),
        )

    late = (
        pltpu.make_async_copy(swap, sw, load_sem.at[8]),
        pltpu.make_async_copy(forth, tf, load_sem.at[9]),
        pltpu.make_async_copy(back, ti, load_sem.at[10]),
        pltpu.make_async_copy(weight, w, load_sem.at[11]),
    )
    for pt in range(4):
        for copy in load_point(pt):
            copy.start()
    for copy in late:
        copy.start()

    barrier = pltpu.get_barrier_semaphore()

    def greet(i, _):
        pl.semaphore_signal(barrier, inc=1, device_id=partner(i), device_id_type=pl.DeviceIdType.MESH)
        return 0

    lax.fori_loop(1, 128, greet, 0)

    lane = lax.broadcasted_iota(jnp.int32, (128, 512), 1)
    slot = lax.broadcasted_iota(jnp.int32, (128, 512), 0)
    spread = (slot == (lane // 32) * 8 + lane % 8).astype(F32).astype(BF)
    blocks = jnp.broadcast_to(order[...].astype(F32), (8, 128)).astype(BF)
    target = dot(blocks, spread)[0:1] * 4.0
    lane1 = lax.broadcasted_iota(jnp.int32, (1, 512), 1)
    target = target + ((lane1 // 8) % 4).astype(F32)
    index = lax.broadcasted_iota(jnp.int32, (512, 512), 0).astype(F32)
    onehot = jnp.where(index == target, 1.0, 0.0)
    cols[...] = onehot.astype(BF)
    rows[...] = onehot.T.astype(BF)

    def make_first(pt, _):
        for copy in load_point(pt):
            copy.wait()
        gr, gi = g[pt, 0], g[pt, 1]
        real = dot(gr, s[pt, 0]) - dot(gi, s[pt, 1])
        imag = dot(gr, s[pt, 1]) + dot(gi, s[pt, 0])
        both = jnp.concatenate([real.astype(BF), imag.astype(BF)], axis=1)
        placed = dot(rows[...], both)
        first[pt, 0] = placed[:, :512].astype(BF)
        first[pt, 1] = placed[:, 512:].astype(BF)
        return 0

    lax.fori_loop(0, 4, make_first, 0)
    late[0].wait()
    pl.semaphore_wait(barrier, 127)

    def outward(chunk, _):
        here = pl.ds(pl.multiple_of(chunk * WIDE, WIDE), WIDE)

        def make_green(pt, _):
            side = g[pt, :, here, :].reshape(2 * WIDE, 512)
            a = dot_t(first[pt, 0], side)
            b = dot_t(first[pt, 1], side)
            gbuf[2 * pt] = (a[:, :WIDE] + b[:, WIDE:]).astype(BF)
            gbuf[2 * pt + 1] = (b[:, :WIDE] - a[:, WIDE:]).astype(BF)
            return 0

        lax.fori_loop(0, 4, make_green, 0)

        def weave(group, _):
            both = [
                gbuf[:, pl.ds(pl.multiple_of((2 * group + h) * 32, 32), 32), :].reshape(256, 128)
                for h in range(2)
            ]
            woven = dot(sw[...], jnp.concatenate(both, axis=1)).astype(BF)
            for h in range(2):
                piece = woven[:, 128 * h : 128 * (h + 1)].reshape(8, 32, 128)
                stage1[chunk, pl.ds((2 * group + h) * 8, 8)] = piece
            return 0

        lax.fori_loop(0, 8, weave, 0)

        def send(i, _):
            to = partner(i)
            pltpu.make_async_remote_copy(
                stage1.at[chunk, to[0] * 8 + to[1]],
                got1.at[chunk, me],
                send1.at[chunk],
                recv1.at[chunk],
                device_id=to,
                device_id_type=pl.DeviceIdType.MESH,
            ).start()
            return 0

        lax.fori_loop(1, 128, send, 0)
        got1[chunk, me] = stage1[chunk, me]
        return 0

    lax.fori_loop(0, CHUNKS, outward, 0)

    def make_gcol(pt, _):
        for part in range(2):
            gcol[pt, part] = dot(g[pt, part], cols[...]).astype(BF)
        return 0

    lax.fori_loop(0, 4, make_gcol, 0)
    for copy in late[1:]:
        copy.wait()

    some = pl.ds(0, 127)

    def convolve(chunk, _):
        pltpu.make_async_copy(stage1.at[chunk, some], got1.at[chunk, some], recv1.at[chunk]).wait()
        for pair in range(2):
            held = got1[chunk, :, 16 * pair : 16 * pair + 16, :].astype(F32)
            held = held.reshape(2, 8, 2, 4, 16, 128)
            plus = held[0] + held[1]
            minus = held[0] - held[1]
            parts = (
                plus[:, 0] + plus[:, 1],
                plus[:, 0] - plus[:, 1],
                minus[:, 0] + minus[:, 1],
                minus[:, 0] - minus[:, 1],
            )
            done = []
            for kind in range(4):
                x = parts[kind]
                x = jnp.concatenate(
                    [x[:, :, 0:8].reshape(256, 128), x[:, :, 8:16].reshape(256, 128)], axis=1
                ).astype(BF)
                y = dot(tf[kind], x)
                lanes = [
                    pl.ds(pl.multiple_of((2 * pair + h) * 512 + chunk * WIDE, WIDE), WIDE)
                    for h in range(2)
                ]
                wr = jnp.concatenate([w[kind, 0, :, at] for at in lanes], axis=1).astype(F32)
                wi = jnp.concatenate([w[kind, 1, :, at] for at in lanes], axis=1).astype(F32)
                yr, yi = y[:128], y[128:]
                z = jnp.concatenate([yr * wr - yi * wi, yr * wi + yi * wr], axis=0).astype(BF)
                done.append(dot(ti[kind], z))
            up, down = done[0] + done[1], done[2] + done[3]
            cross_up, cross_down = done[0] - done[1], done[2] - done[3]
            results = ((up + down, cross_up + cross_down), (up - down, cross_up - cross_down))
            for eh in range(2):
                for mh in range(2):
                    x = results[eh][mh]
                    x = jnp.concatenate(
                        [x[:, :128].reshape(8, 4, 8, 128), x[:, 128:].reshape(8, 4, 8, 128)], axis=2
                    ).astype(BF)
                    for low in range(8):
                        at = (8 * eh + low) * 8 + 4 * mh
                        stage2[chunk, at : at + 4, 16 * pair : 16 * pair + 16, :] = x[low]

        def send(i, _):
            to = partner(i)
            pltpu.make_async_remote_copy(
                stage2.at[chunk, to[0] * 8 + to[1]],
                got2.at[chunk, me],
                send2.at[chunk],
                recv2.at[chunk],
                device_id=to,
                device_id_type=pl.DeviceIdType.MESH,
            ).start()
            return 0

        lax.fori_loop(1, 128, send, 0)
        got2[chunk, me] = stage2[chunk, me]
        return 0

    lax.fori_loop(0, CHUNKS, convolve, 0)

    for half in range(2):

        def inward(chunk, _):
            here = pl.ds(pl.multiple_of(chunk * WIDE, WIDE), WIDE)
            pltpu.make_async_copy(stage2.at[chunk, some], got2.at[chunk, some], recv2.at[chunk]).wait()

            def unweave(group, _):
                both = [
                    got2[chunk, pl.ds((2 * group + h) * 8, 8)].reshape(256, 128) for h in range(2)
                ]
                parted = dot(sw[...], jnp.concatenate(both, axis=1)).astype(BF)
                for h in range(2):
                    at = pl.ds(pl.multiple_of((2 * group + h) * 32, 32), 32)
                    for part in range(2):
                        sig[:, at, part * 128 : part * 128 + 128] = parted[
                            :, 128 * h : 128 * (h + 1)
                        ].reshape(4, 2, 32, 128)[:, part]
                return 0

            lax.fori_loop(0, 8, unweave, 0)

            def make_first2(pt, _):
                a = dot(gcol[pt, 0], sig[pt])
                b = dot(gcol[pt, 1], sig[pt])
                first[pt, 0, :, here] = (a[:, :WIDE] - b[:, WIDE:]).astype(BF)
                first[pt, 1, :, here] = (a[:, WIDE:] + b[:, :WIDE]).astype(BF)
                return 0

            lax.fori_loop(0, 4, make_first2, 0)
            return 0

        lax.fori_loop(2 * half, 2 * half + 2, inward, 0)
        span = slice(256 * half, 256 * half + 256)

        def finish(pt, _):
            fr, fi = first[pt, 0, :, span], first[pt, 1, :, span]
            gr, gi = g[pt, 0, :, span], g[pt, 1, :, span]
            real = dot_t(fr, gr) + dot_t(fi, gi)
            imag = dot_t(fi, gr) - dot_t(fr, gi)
            if half == 0:
                acc[pt, 0] = real
                acc[pt, 1] = imag
            else:
                s[pt, 0] = (acc[pt, 0] + real).astype(BF)
                s[pt, 1] = (acc[pt, 1] + imag).astype(BF)
                pltpu.make_async_copy(s.at[pt], out.at[pt], out_sem.at[pt]).start()
            return 0

        lax.fori_loop(0, 4, finish, 0)

    for chunk in range(CHUNKS):
        pltpu.make_async_copy(stage1.at[chunk, some], got1.at[chunk, some], send1.at[chunk]).wait()
        pltpu.make_async_copy(stage2.at[chunk, some], got2.at[chunk, some], send2.at[chunk]).wait()
    for pt in range(4):
        pltpu.make_async_copy(s.at[pt], out.at[pt], out_sem.at[pt]).wait()


def local(green_ret, sigma_in, screened, block_of_slot):
    forth, back = transforms()
    weight = screened.reshape(16, 2, 8, 2, 2, 2048).transpose(1, 3, 4, 0, 2, 5).reshape(4, 2, 128, 2048)
    hbm = pl.BlockSpec(memory_space=pl.ANY)
    exchange = pltpu.VMEM((CHUNKS, 128, 32, 128), BF)
    result = pl.pallas_call(
        kernel,
        out_shape=jax.ShapeDtypeStruct((4, 2, 512, 512), BF),
        in_specs=[pl.BlockSpec(memory_space=pltpu.VMEM)] + [hbm] * 6,
        out_specs=hbm,
        scratch_shapes=[
            pltpu.VMEM((4, 2, 512, 512), BF),
            pltpu.VMEM((4, 2, 512, 512), BF),
            pltpu.VMEM((4, 2, 128, 2048), BF),
            pltpu.VMEM((4, 256, 256), BF),
            pltpu.VMEM((4, 256, 256), BF),
            pltpu.VMEM((256, 256), BF),
            pltpu.VMEM((512, 512), BF),
            pltpu.VMEM((512, 512), BF),
            pltpu.VMEM((4, 2, 512, 512), BF),
            pltpu.VMEM((8, 512, 128), BF),
            pltpu.VMEM((4, 2, 512, 512), BF),
            exchange,
            exchange,
            exchange,
            exchange,
            pltpu.VMEM((4, 512, 256), BF),
            pltpu.VMEM((4, 2, 512, 512), F32),
            pltpu.SemaphoreType.DMA((12,)),
            pltpu.SemaphoreType.DMA((CHUNKS,)),
            pltpu.SemaphoreType.DMA((CHUNKS,)),
            pltpu.SemaphoreType.DMA((CHUNKS,)),
            pltpu.SemaphoreType.DMA((CHUNKS,)),
            pltpu.SemaphoreType.DMA((4,)),
        ],
        compiler_params=pltpu.CompilerParams(
            collective_id=0, has_side_effects=True, vmem_limit_bytes=60 << 20
        ),
    )(
        block_of_slot.reshape(1, 128),
        green_ret.reshape(4, 2, 512, 512),
        sigma_in.reshape(4, 2, 512, 512),
        weight,
        forth,
        back,
        swapper(),
    )
    return result.reshape(2, 2, 2, 512, 512)


def solution(mesh):
    in_specs = (
        P("energy", "momentum", None, None, None),
        P("energy", "momentum", None, None, None),
        P(("energy", "momentum"), None, None, None, None),
        P(),
    )
    out_specs = P("energy", "momentum", None, None, None)
    return jax.shard_map(local, mesh=mesh, in_specs=in_specs, out_specs=out_specs, check_vma=False)
```

```python
import jax
import jax.numpy as jnp
import numpy as np
from jax import lax
from jax.experimental import pallas as pl
from jax.experimental.pallas import tpu as pltpu
from jax.sharding import PartitionSpec as P

BF = jnp.bfloat16
F32 = jnp.float32
CHUNKS = 4
WIDE = 128


def transforms():
    m, n = np.arange(16), np.arange(8)
    e, k = np.arange(16), np.arange(8)
    out = np.zeros((4, 256, 256), np.float64)
    for a in range(2):
        for b in range(2):
            steps = ((2 * m + a)[:, None, None, None] * e[None, None, :, None]) * 1.0 / 32
            steps = steps + ((2 * n + b)[None, :, None, None] * k[None, None, None, :]) * 1.0 / 16
            cos, sin = np.cos(2 * np.pi * steps), np.sin(2 * np.pi * steps)
            cols = np.zeros((2, 16, 8, 16, 8, 2))
            cols[0, ..., 0], cols[0, ..., 1] = cos, sin
            cols[1, ..., 0], cols[1, ..., 1] = -sin, cos
            cols = cols.reshape(2, 16, 8, 8, 2, 4, 2, 2).transpose(0, 1, 2, 3, 5, 4, 6, 7)
            out[2 * a + b] = cols.reshape(256, 256)
    back = out.transpose(0, 2, 1) / 512
    return jnp.asarray(out, BF), jnp.asarray(back, BF)


def weaver():
    row = np.arange(256)
    taken = (row % 8) * 32 + row // 8
    return np.arange(256)[None, :] == taken[:, None]


def splitter():
    row = np.arange(256)
    kind, part, m, n = row // 64, row // 32 % 2, row // 8 % 4, row % 8
    taken = ((2 * m + kind // 2) * 16 + 2 * n + kind % 2) * 2 + part
    return np.arange(256)[None, :] == taken[:, None]


def orders():
    return jnp.asarray(np.stack([weaver(), weaver().T, splitter()]), BF)


def dot(a, b):
    return jnp.dot(a, b, preferred_element_type=F32)


def dot_t(a, b):
    return lax.dot_general(a, b, (((1,), (1,)), ((), ())), preferred_element_type=F32)


def beside(a, b):
    return jnp.concatenate([a, b], axis=1)


def above(a, b):
    return jnp.concatenate([a, b], axis=0)


def kernel(
    order, order_row, green, sigma, screened, forth, back, moves, out,
    g, s, raw, w, tf, ti, mv, cols, first, gbuf, woven, gcol, stage1, got1, stage2, got2, sig, acc,
    load_sem, send1, recv1, send2, recv2, out_sem,
):
    e = lax.axis_index("energy")
    m = lax.axis_index("momentum")
    me = e * 8 + m
    my_z, my_y, my_x, my_core = e // 4, (m // 4) * 2 + (e // 2) % 2, m % 4, e % 2
    ys = [(my_y + i) % 4 for i in range(4)]
    zs = [(my_z + i) % 4 for i in range(4)]
    near = []
    for y in range(4):
        for z in range(4):
            for core in range(2):
                to_core = my_core if core == 0 else 1 - my_core
                near.append((zs[z] * 4 + (ys[y] % 2) * 2 + to_core, (ys[y] // 2) * 4))

    def each_partner(act):
        def at_x(x, _):
            xs = [(my_x + x + i) % 4 for i in range(4)]
            for k in range(32):
                to = (near[k][0], near[k][1] + xs[(k // 8 + k // 2) % 4])
                if k == 0:
                    pl.when(x > 0)(lambda to=to: act(to))
                else:
                    act(to)
            return 0

        lax.fori_loop(0, 4, at_x, 0)

    def load_point(pt):
        return (
            pltpu.make_async_copy(green.at[pt], g.at[pt], load_sem.at[pt]),
            pltpu.make_async_copy(sigma.at[pt], s.at[pt], load_sem.at[4 + pt]),
        )

    late = (
        pltpu.make_async_copy(moves, mv, load_sem.at[8]),
        pltpu.make_async_copy(forth, tf, load_sem.at[9]),
        pltpu.make_async_copy(back, ti, load_sem.at[10]),
    )
    for pt in range(4):
        for copy in load_point(pt):
            copy.start()
    for copy in late:
        copy.start()

    barrier = pltpu.get_barrier_semaphore()
    each_partner(
        lambda to: pl.semaphore_signal(
            barrier, inc=1, device_id=to, device_id_type=pl.DeviceIdType.MESH
        )
    )

    def make_first(pt, _):
        for copy in load_point(pt):
            copy.wait()
        sr, si = s[pt, 0], s[pt, 1]
        first[pt] = dot(beside(g[pt, 0], g[pt, 1]), above(beside(sr, si), beside(-si, sr))).astype(BF)
        return 0

    lax.fori_loop(0, 4, make_first, 0)
    late[0].wait()
    pl.semaphore_wait(barrier, 127)

    def outward(chunk, _):
        here = pl.ds(pl.multiple_of(chunk * WIDE, WIDE), WIDE)

        def make_green(pt, _):
            gr, gi = g[pt, 0, here, :], g[pt, 1, here, :]
            both = dot_t(first[pt], above(beside(gr, gi), beside(-gi, gr))).astype(BF)
            gbuf[2 * pt] = both[:, :WIDE]
            gbuf[2 * pt + 1] = both[:, WIDE:]
            return 0

        lax.fori_loop(0, 4, make_green, 0)

        def weave(group, _):
            both = [
                gbuf[:, pl.ds(pl.multiple_of((2 * group + h) * 32, 32), 32), :].reshape(256, 128)
                for h in range(2)
            ]
            mixed = dot(mv[0], beside(*both)).astype(BF)
            for h in range(2):
                piece = mixed[:, 128 * h : 128 * (h + 1)].reshape(8, 32, 128)
                woven[pl.ds((2 * group + h) * 8, 8)] = piece
            return 0

        lax.fori_loop(0, 8, weave, 0)

        def send(to):
            slot = to[0] * 8 + to[1]
            stage1[chunk, slot] = woven[order[slot]]
            pltpu.make_async_remote_copy(
                stage1.at[chunk, slot],
                got1.at[chunk, me],
                send1.at[chunk],
                recv1.at[chunk],
                device_id=to,
                device_id_type=pl.DeviceIdType.MESH,
            ).start()

        each_partner(send)
        got1[chunk, me] = woven[order[me]]
        return 0

    lax.fori_loop(0, CHUNKS, outward, 0)

    lane = lax.broadcasted_iota(jnp.int32, (128, 512), 1)
    slot = lax.broadcasted_iota(jnp.int32, (128, 512), 0)
    spread = (slot == lane // 4).astype(F32).astype(BF)
    blocks = jnp.broadcast_to(order_row[...].astype(F32), (8, 128)).astype(BF)
    lane1 = lax.broadcasted_iota(jnp.int32, (1, 512), 1)
    target = dot(blocks, spread)[0:1] * 4.0 + (lane1 % 4).astype(F32)
    index = lax.broadcasted_iota(jnp.int32, (512, 512), 0).astype(F32)
    cols[...] = jnp.where(index == target, 1.0, 0.0).astype(BF)

    def make_gcol(pt, _):
        for part in range(2):
            gcol[pt, :, 512 * part : 512 * part + 512] = dot(g[pt, part], cols[...]).astype(BF)
        return 0

    lax.fori_loop(0, 4, make_gcol, 0)

    def split(group, _):
        load = pltpu.make_async_copy(screened.at[pl.ds(group * 8, 8)], raw, load_sem.at[11])
        load.start()
        load.wait()
        parted = dot(mv[2], raw[...].reshape(256, 2048)).astype(BF)
        w[:, :, pl.ds(pl.multiple_of(group * 32, 32), 32), :] = parted.reshape(4, 2, 32, 2048)
        return 0

    lax.fori_loop(0, 4, split, 0)
    for copy in late[1:]:
        copy.wait()

    some = pl.ds(0, 127)

    def convolve(chunk, _):
        pltpu.make_async_copy(stage1.at[chunk, some], got1.at[chunk, some], recv1.at[chunk]).wait()
        for pair in range(2):
            held = got1[chunk, :, 16 * pair : 16 * pair + 16, :].astype(F32)
            held = held.reshape(2, 8, 2, 4, 16, 128)
            plus = held[0] + held[1]
            minus = held[0] - held[1]
            parts = (
                plus[:, 0] + plus[:, 1],
                plus[:, 0] - plus[:, 1],
                minus[:, 0] + minus[:, 1],
                minus[:, 0] - minus[:, 1],
            )
            done = []
            for kind in range(4):
                x = parts[kind]
                x = beside(x[:, :, 0:8].reshape(256, 128), x[:, :, 8:16].reshape(256, 128))
                y = dot(tf[kind], x.astype(BF))
                lanes = [
                    pl.ds(pl.multiple_of((2 * pair + h) * 512 + chunk * WIDE, WIDE), WIDE)
                    for h in range(2)
                ]
                wr = beside(*[w[kind, 0, :, at] for at in lanes]).astype(F32)
                wi = beside(*[w[kind, 1, :, at] for at in lanes]).astype(F32)
                yr, yi = y[:128], y[128:]
                z = above(yr * wr - yi * wi, yr * wi + yi * wr).astype(BF)
                done.append(dot(ti[kind], z))
            up, down = done[0] + done[1], done[2] + done[3]
            cross_up, cross_down = done[0] - done[1], done[2] - done[3]
            results = ((up + down, cross_up + cross_down), (up - down, cross_up - cross_down))
            for eh in range(2):
                for mh in range(2):
                    x = results[eh][mh]
                    x = jnp.concatenate(
                        [x[:, :128].reshape(8, 4, 8, 128), x[:, 128:].reshape(8, 4, 8, 128)], axis=2
                    ).astype(BF)
                    for low in range(8):
                        at = (8 * eh + low) * 8 + 4 * mh
                        stage2[chunk, at : at + 4, 16 * pair : 16 * pair + 16, :] = x[low]

        def send(to):
            pltpu.make_async_remote_copy(
                stage2.at[chunk, to[0] * 8 + to[1]],
                got2.at[chunk, me],
                send2.at[chunk],
                recv2.at[chunk],
                device_id=to,
                device_id_type=pl.DeviceIdType.MESH,
            ).start()

        each_partner(send)
        got2[chunk, me] = stage2[chunk, me]
        return 0

    lax.fori_loop(0, CHUNKS, convolve, 0)

    for chunk in range(CHUNKS):
        span = slice(WIDE * chunk, WIDE * chunk + WIDE)
        pltpu.make_async_copy(stage2.at[chunk, some], got2.at[chunk, some], recv2.at[chunk]).wait()

        def unweave(group, _):
            both = [got2[chunk, pl.ds((2 * group + h) * 8, 8)].reshape(256, 128) for h in range(2)]
            parted = dot(mv[1], beside(*both)).astype(BF)
            for h in range(2):
                at = pl.ds(pl.multiple_of((2 * group + h) * 32, 32), 32)
                piece = parted[:, 128 * h : 128 * (h + 1)].reshape(4, 2, 32, 128)
                sig[:, 0, at, :] = piece[:, 0]
                sig[:, 1, at, :] = piece[:, 1]
            return 0

        lax.fori_loop(0, 8, unweave, 0)

        def inward(pt, _):
            sr, si = sig[pt, 0], sig[pt, 1]
            mine = dot(gcol[pt], above(beside(sr, si), beside(-si, sr))).astype(BF)
            gr, gi = g[pt, 0, :, span], g[pt, 1, :, span]
            part = dot_t(mine, above(beside(gr, gi), beside(-gi, gr)))
            if chunk > 0:
                part = part + acc[pt]
            if chunk < CHUNKS - 1:
                acc[pt] = part
            else:
                part = part.astype(BF)
                s[pt, 0] = part[:, :512]
                s[pt, 1] = part[:, 512:]
                pltpu.make_async_copy(s.at[pt], out.at[pt], out_sem.at[pt]).start()
            return 0

        lax.fori_loop(0, 4, inward, 0)

    for chunk in range(CHUNKS):
        pltpu.make_async_copy(stage1.at[chunk, some], got1.at[chunk, some], send1.at[chunk]).wait()
        pltpu.make_async_copy(stage2.at[chunk, some], got2.at[chunk, some], send2.at[chunk]).wait()
    for pt in range(4):
        pltpu.make_async_copy(s.at[pt], out.at[pt], out_sem.at[pt]).wait()


def local(green_ret, sigma_in, screened, block_of_slot):
    forth, back = transforms()
    hbm = pl.BlockSpec(memory_space=pl.ANY)
    exchange = pltpu.VMEM((CHUNKS, 128, 32, 128), BF)
    result = pl.pallas_call(
        kernel,
        out_shape=jax.ShapeDtypeStruct((4, 2, 512, 512), BF),
        in_specs=[pl.BlockSpec(memory_space=pltpu.SMEM), pl.BlockSpec(memory_space=pltpu.VMEM)]
        + [hbm] * 6,
        out_specs=hbm,
        scratch_shapes=[
            pltpu.VMEM((4, 2, 512, 512), BF),
            pltpu.VMEM((4, 2, 512, 512), BF),
            pltpu.VMEM((8, 16, 2, 2048), BF),
            pltpu.VMEM((4, 2, 128, 2048), BF),
            pltpu.VMEM((4, 256, 256), BF),
            pltpu.VMEM((4, 256, 256), BF),
            pltpu.VMEM((3, 256, 256), BF),
            pltpu.VMEM((512, 512), BF),
            pltpu.VMEM((4, 512, 1024), BF),
            pltpu.VMEM((8, 512, 128), BF),
            pltpu.VMEM((128, 32, 128), BF),
            pltpu.VMEM((4, 512, 1024), BF),
            exchange,
            exchange,
            exchange,
            exchange,
            pltpu.VMEM((4, 2, 512, 128), BF),
            pltpu.VMEM((4, 512, 1024), F32),
            pltpu.SemaphoreType.DMA((12,)),
            pltpu.SemaphoreType.DMA((CHUNKS,)),
            pltpu.SemaphoreType.DMA((CHUNKS,)),
            pltpu.SemaphoreType.DMA((CHUNKS,)),
            pltpu.SemaphoreType.DMA((CHUNKS,)),
            pltpu.SemaphoreType.DMA((4,)),
        ],
        compiler_params=pltpu.CompilerParams(
            collective_id=0, has_side_effects=True, vmem_limit_bytes=56 << 20
        ),
    )(
        block_of_slot,
        block_of_slot.reshape(1, 128),
        green_ret.reshape(4, 2, 512, 512),
        sigma_in.reshape(4, 2, 512, 512),
        screened.reshape(32, 16, 2, 2048),
        forth,
        back,
        orders(),
    )
    return result.reshape(2, 2, 2, 512, 512)


def solution(mesh):
    in_specs = (
        P("energy", "momentum", None, None, None),
        P("energy", "momentum", None, None, None),
        P(("energy", "momentum"), None, None, None, None),
        P(),
    )
    out_specs = P("energy", "momentum", None, None, None)
    return jax.shard_map(local, mesh=mesh, in_specs=in_specs, out_specs=out_specs, check_vma=False)
```

```python
import jax
import jax.numpy as jnp
import numpy as np
from jax import lax
from jax.experimental import pallas as pl
from jax.experimental.pallas import tpu as pltpu
from jax.sharding import PartitionSpec as P

BF = jnp.bfloat16
F32 = jnp.float32
CHUNKS = 4
WIDE = 128


def transforms():
    m, n = np.arange(16), np.arange(8)
    e, k = np.arange(16), np.arange(8)
    out = np.zeros((4, 256, 256), np.float64)
    for a in range(2):
        for b in range(2):
            steps = ((2 * m + a)[:, None, None, None] * e[None, None, :, None]) * 1.0 / 32
            steps = steps + ((2 * n + b)[None, :, None, None] * k[None, None, None, :]) * 1.0 / 16
            cos, sin = np.cos(2 * np.pi * steps), np.sin(2 * np.pi * steps)
            cols = np.zeros((2, 16, 8, 16, 8, 2))
            cols[0, ..., 0], cols[0, ..., 1] = cos, sin
            cols[1, ..., 0], cols[1, ..., 1] = -sin, cos
            cols = cols.reshape(2, 16, 8, 8, 2, 4, 2, 2).transpose(0, 1, 2, 3, 5, 4, 6, 7)
            out[2 * a + b] = cols.reshape(256, 256)
    return out


def weaver():
    row = np.arange(256)
    taken = (row % 8) * 32 + row // 8
    return np.arange(256)[None, :] == taken[:, None]


def splitter():
    row = np.arange(256)
    kind, part, m, n = row // 64, row // 32 % 2, row // 8 % 4, row % 8
    taken = ((2 * m + kind // 2) * 16 + 2 * n + kind % 2) * 2 + part
    return np.arange(256)[None, :] == taken[:, None]


def half_weaver():
    row = np.arange(256)
    taken = (row % 4) * 64 + row // 4
    return np.arange(256)[None, :] == taken[:, None]


def joiner():
    row = np.arange(256)
    taken = (row // 4 % 2) * 128 + (row // 32) * 16 + (row // 8 % 4) * 4 + row % 4
    return np.arange(256)[None, :] == taken[:, None]


FORTH, BACK, WEAVE, UNWEAVE, SPLIT, HALF_WEAVE, HALF_UNWEAVE, JOIN, PART = 0, 4, 8, 9, 10, 11, 12, 13, 14
MATRICES, ROOM = 15, 40


def matrices():
    forth = transforms()
    moves = [weaver(), weaver().T, splitter(), half_weaver(), half_weaver().T, joiner(), joiner().T]
    spare = np.zeros((ROOM - MATRICES, 256, 256))
    return jnp.asarray(np.concatenate([forth, forth.transpose(0, 2, 1) / 512, np.stack(moves), spare]), BF)


def dot(a, b):
    return jnp.dot(a, b, preferred_element_type=F32)


def dot_t(a, b):
    return lax.dot_general(a, b, (((1,), (1,)), ((), ())), preferred_element_type=F32)


def beside(a, b):
    return jnp.concatenate([a, b], axis=1)


def above(a, b):
    return jnp.concatenate([a, b], axis=0)


def kernel(
    order, order_row, green, sigma, screened, tables, out,
    g, s, raw, mv, cols, first, gbuf, woven, half_woven, stage, got1, got2, sig, acc,
    half_stage, half_got, last_got, load_sem, send1, recv1, send2, recv2, half_sem, out_sem,
):
    e = lax.axis_index("energy")
    m = lax.axis_index("momentum")
    me = e * 8 + m
    my_z, my_y, my_x, my_core = e // 4, (m // 4) * 2 + (e // 2) % 2, m % 4, e % 2
    ys = [(my_y + i) % 4 for i in range(4)]
    zs = [(my_z + i) % 4 for i in range(4)]
    near = []
    for y in range(4):
        for z in range(4):
            for core in range(2):
                to_core = my_core if core == 0 else 1 - my_core
                near.append((zs[z] * 4 + (ys[y] % 2) * 2 + to_core, (ys[y] // 2) * 4))

    def each_partner(act):
        def at_x(x, _):
            xs = [(my_x + x + i) % 4 for i in range(4)]
            for k in range(32):
                to = (near[k][0], near[k][1] + xs[(k // 8 + k // 2) % 4])
                if k == 0:
                    pl.when(x > 0)(lambda to=to: act(to))
                else:
                    act(to)
            return 0

        lax.fori_loop(0, 4, at_x, 0)

    def load_point(pt):
        return (
            pltpu.make_async_copy(green.at[pt], g.at[pt], load_sem.at[pt]),
            pltpu.make_async_copy(sigma.at[pt], s.at[pt], load_sem.at[4 + pt]),
        )

    late = pltpu.make_async_copy(tables.at[pl.ds(0, MATRICES)], mv, load_sem.at[8])
    for pt in range(4):
        for copy in load_point(pt):
            copy.start()
    late.start()

    barrier = pltpu.get_barrier_semaphore()
    each_partner(
        lambda to: pl.semaphore_signal(
            barrier, inc=1, device_id=to, device_id_type=pl.DeviceIdType.MESH
        )
    )

    def make_first(pt, _):
        for copy in load_point(pt):
            copy.wait()
        sr, si = s[pt, 0], s[pt, 1]
        first[pt] = dot(beside(g[pt, 0], g[pt, 1]), above(beside(sr, si), beside(-si, sr))).astype(BF)
        return 0

    def green_of(chunk):
        here = pl.ds(pl.multiple_of(chunk * WIDE, WIDE), WIDE)

        def make_green(pt, _):
            gr, gi = g[pt, 0, here, :], g[pt, 1, here, :]
            both = dot_t(first[pt], above(beside(gr, gi), beside(-gi, gr))).astype(BF)
            gbuf[2 * pt] = both[:, :WIDE]
            gbuf[2 * pt + 1] = both[:, WIDE:]
            return 0

        return make_green

    for half in range(2):
        lax.fori_loop(2 * half, 2 * half + 2, make_first, 0)
        lax.fori_loop(2 * half, 2 * half + 2, green_of(0), 0)
        if half == 0:
            late.wait()

        def half_weave(group, _):
            both = [
                gbuf[
                    4 * half : 4 * half + 4, pl.ds(pl.multiple_of((2 * group + h) * 64, 64), 64), :
                ].reshape(256, 128)
                for h in range(2)
            ]
            mixed = dot(mv[HALF_WEAVE], beside(*both)).astype(BF)
            for h in range(2):
                piece = mixed[:, 128 * h : 128 * (h + 1)].reshape(16, 16, 128)
                half_woven[pl.ds((2 * group + h) * 16, 16)] = piece
            return 0

        lax.fori_loop(0, 4, half_weave, 0)
        if half == 0:
            pl.semaphore_wait(barrier, 127)

        def send_half(to):
            slot = to[0] * 8 + to[1]
            half_stage[half, slot] = half_woven[order[slot]]
            pltpu.make_async_remote_copy(
                half_stage.at[half, slot],
                half_got.at[half, me],
                half_sem.at[half],
                half_sem.at[2 + half],
                device_id=to,
                device_id_type=pl.DeviceIdType.MESH,
            ).start()

        each_partner(send_half)
        half_got[half, me] = half_woven[order[me]]

    def outward(chunk, _):
        lax.fori_loop(0, 4, green_of(chunk), 0)

        def weave(group, _):
            both = [
                gbuf[:, pl.ds(pl.multiple_of((2 * group + h) * 32, 32), 32), :].reshape(256, 128)
                for h in range(2)
            ]
            mixed = dot(mv[WEAVE], beside(*both)).astype(BF)
            for h in range(2):
                piece = mixed[:, 128 * h : 128 * (h + 1)].reshape(8, 32, 128)
                woven[pl.ds((2 * group + h) * 8, 8)] = piece
            return 0

        lax.fori_loop(0, 8, weave, 0)

        def send(to):
            slot = to[0] * 8 + to[1]
            stage[chunk, slot] = woven[order[slot]]
            pltpu.make_async_remote_copy(
                stage.at[chunk, slot],
                got1.at[chunk, me],
                send1.at[chunk],
                recv1.at[chunk],
                device_id=to,
                device_id_type=pl.DeviceIdType.MESH,
            ).start()

        each_partner(send)
        got1[chunk, me] = woven[order[me]]
        return 0

    lax.fori_loop(1, CHUNKS, outward, 0)

    lane = lax.broadcasted_iota(jnp.int32, (128, 512), 1)
    slot = lax.broadcasted_iota(jnp.int32, (128, 512), 0)
    spread = (slot == lane // 4).astype(F32).astype(BF)
    blocks = jnp.broadcast_to(order_row[...].astype(F32), (8, 128)).astype(BF)
    lane1 = lax.broadcasted_iota(jnp.int32, (1, 512), 1)
    target = dot(blocks, spread)[0:1] * 4.0 + (lane1 % 4).astype(F32)
    index = lax.broadcasted_iota(jnp.int32, (512, 512), 0).astype(F32)
    cols[...] = jnp.where(index == target, 1.0, 0.0).astype(BF)

    def make_gcol(pt, _):
        for part in range(2):
            first[pt, :, 512 * part : 512 * part + 512] = dot(g[pt, part], cols[...]).astype(BF)
        return 0

    lax.fori_loop(0, 4, make_gcol, 0)

    def split(group, _):
        load = pltpu.make_async_copy(screened.at[pl.ds(group * 8, 8)], raw, load_sem.at[11])
        load.start()
        load.wait()
        parted = dot(mv[SPLIT], raw[...].reshape(256, 2048)).astype(BF)
        for row in range(4):
            at = pl.ds(pl.multiple_of(row * 128 + group * 32, 32), 32)
            s[:, :, at, :] = parted[:, 512 * row : 512 * row + 512].reshape(4, 2, 32, 512)
        return 0

    lax.fori_loop(0, 4, split, 0)

    some = pl.ds(0, 127)

    def whole(half, sem):
        return pltpu.make_async_copy(
            half_stage.at[half, some], half_got.at[half, some], half_sem.at[sem + half]
        )

    for half in range(2):
        whole(half, 2).wait()

    def join(group, _):
        both = [
            half_got[:, pl.ds((2 * group + h) * 8, 8)].reshape(256, 128) for h in range(2)
        ]
        mixed = dot(mv[JOIN], beside(*both)).astype(BF)
        for h in range(2):
            piece = mixed[:, 128 * h : 128 * (h + 1)].reshape(8, 32, 128)
            got1[0, pl.ds((2 * group + h) * 8, 8)] = piece
        return 0

    lax.fori_loop(0, 8, join, 0)
    for half in range(2):
        whole(half, 0).wait()

    def convolve(chunk, _):
        @pl.when(chunk > 0)
        def _():
            pltpu.make_async_copy(stage.at[chunk, some], got1.at[chunk, some], recv1.at[chunk]).wait()
            pltpu.make_async_copy(stage.at[chunk, some], got1.at[chunk, some], send1.at[chunk]).wait()

        here = pl.ds(pl.multiple_of(chunk * WIDE, WIDE), WIDE)
        for pair in range(2):
            held = got1[chunk, :, 16 * pair : 16 * pair + 16, :].astype(F32)
            held = held.reshape(2, 8, 2, 4, 16, 128)
            plus = held[0] + held[1]
            minus = held[0] - held[1]
            parts = (
                plus[:, 0] + plus[:, 1],
                plus[:, 0] - plus[:, 1],
                minus[:, 0] + minus[:, 1],
                minus[:, 0] - minus[:, 1],
            )
            done = []
            for kind in range(4):
                x = parts[kind]
                x = beside(x[:, :, 0:8].reshape(256, 128), x[:, :, 8:16].reshape(256, 128))
                y = dot(mv[FORTH + kind], x.astype(BF))
                spans = [pl.ds((2 * pair + h) * 128, 128) for h in range(2)]
                wr = beside(*[s[kind, 0, at, here] for at in spans]).astype(F32)
                wi = beside(*[s[kind, 1, at, here] for at in spans]).astype(F32)
                yr, yi = y[:128], y[128:]
                z = above(yr * wr - yi * wi, yr * wi + yi * wr).astype(BF)
                done.append(dot(mv[BACK + kind], z))
            up, down = done[0] + done[1], done[2] + done[3]
            cross_up, cross_down = done[0] - done[1], done[2] - done[3]
            results = ((up + down, cross_up + cross_down), (up - down, cross_up - cross_down))
            for eh in range(2):
                for mh in range(2):
                    x = results[eh][mh]
                    x = jnp.concatenate(
                        [x[:, :128].reshape(8, 4, 8, 128), x[:, 128:].reshape(8, 4, 8, 128)], axis=2
                    ).astype(BF)
                    for low in range(8):
                        at = (8 * eh + low) * 8 + 4 * mh
                        stage[chunk, at : at + 4, 16 * pair : 16 * pair + 16, :] = x[low]

        def send(to):
            pltpu.make_async_remote_copy(
                stage.at[chunk, to[0] * 8 + to[1]],
                got2.at[chunk, me],
                send2.at[chunk],
                recv2.at[chunk],
                device_id=to,
                device_id_type=pl.DeviceIdType.MESH,
            ).start()

        @pl.when(chunk < CHUNKS - 1)
        def _():
            each_partner(send)
            got2[chunk, me] = stage[chunk, me]

        return 0

    lax.fori_loop(0, CHUNKS, convolve, 0)

    def part(group, _):
        both = [
            stage[CHUNKS - 1, pl.ds((2 * group + h) * 8, 8)].reshape(256, 128) for h in range(2)
        ]
        mixed = dot(mv[PART], beside(*both)).astype(BF)
        for h in range(2):
            piece = mixed[:, 128 * h : 128 * (h + 1)].reshape(2, 8, 16, 128)
            half_stage[:, pl.ds((2 * group + h) * 8, 8)] = piece
        return 0

    lax.fori_loop(0, 8, part, 0)
    for half in range(2):

        def send_last(to):
            pltpu.make_async_remote_copy(
                half_stage.at[half, to[0] * 8 + to[1]],
                last_got.at[half, me],
                half_sem.at[4 + half],
                half_sem.at[6 + half],
                device_id=to,
                device_id_type=pl.DeviceIdType.MESH,
            ).start()

        each_partner(send_last)
        last_got[half, me] = half_stage[half, me]

    def inward(chunk):
        span = slice(WIDE * chunk, WIDE * chunk + WIDE)

        def at_point(pt, _):
            sr, si = sig[pt, 0], sig[pt, 1]
            mine = dot(first[pt], above(beside(sr, si), beside(-si, sr))).astype(BF)
            gr, gi = g[pt, 0, :, span], g[pt, 1, :, span]
            total = dot_t(mine, above(beside(gr, gi), beside(-gi, gr)))
            if chunk > 0:
                total = total + acc[pt]
            if chunk < CHUNKS - 1:
                acc[pt] = total
            else:
                total = total.astype(BF)
                s[pt, 0] = total[:, :512]
                s[pt, 1] = total[:, 512:]
                pltpu.make_async_copy(s.at[pt], out.at[pt], out_sem.at[pt]).start()
            return 0

        return at_point

    for chunk in range(CHUNKS - 1):
        pltpu.make_async_copy(stage.at[chunk, some], got2.at[chunk, some], recv2.at[chunk]).wait()

        def unweave(group, _):
            both = [got2[chunk, pl.ds((2 * group + h) * 8, 8)].reshape(256, 128) for h in range(2)]
            parted = dot(mv[UNWEAVE], beside(*both)).astype(BF)
            for h in range(2):
                at = pl.ds(pl.multiple_of((2 * group + h) * 32, 32), 32)
                piece = parted[:, 128 * h : 128 * (h + 1)].reshape(4, 2, 32, 128)
                sig[:, 0, at, :] = piece[:, 0]
                sig[:, 1, at, :] = piece[:, 1]
            return 0

        lax.fori_loop(0, 8, unweave, 0)
        lax.fori_loop(0, 4, inward(chunk), 0)

    for half in range(2):
        whole(half, 6).wait()

        def half_unweave(group, _):
            both = [
                last_got[half, pl.ds((2 * group + h) * 16, 16)].reshape(256, 128) for h in range(2)
            ]
            parted = dot(mv[HALF_UNWEAVE], beside(*both)).astype(BF)
            for h in range(2):
                at = pl.ds(pl.multiple_of((2 * group + h) * 64, 64), 64)
                piece = parted[:, 128 * h : 128 * (h + 1)].reshape(2, 2, 64, 128)
                sig[2 * half : 2 * half + 2, :, at, :] = piece
            return 0

        lax.fori_loop(0, 4, half_unweave, 0)
        lax.fori_loop(2 * half, 2 * half + 2, inward(CHUNKS - 1), 0)

    for chunk in range(CHUNKS - 1):
        pltpu.make_async_copy(stage.at[chunk, some], got2.at[chunk, some], send2.at[chunk]).wait()
    for half in range(2):
        whole(half, 4).wait()
    for pt in range(4):
        pltpu.make_async_copy(s.at[pt], out.at[pt], out_sem.at[pt]).wait()


def local(green_ret, sigma_in, screened, block_of_slot):
    hbm = pl.BlockSpec(memory_space=pltpu.HBM)
    exchange = pltpu.VMEM((CHUNKS, 128, 32, 128), BF)
    halves = pltpu.VMEM((2, 128, 16, 128), BF)
    result = pl.pallas_call(
        kernel,
        out_shape=jax.ShapeDtypeStruct((4, 2, 512, 512), BF),
        in_specs=[pl.BlockSpec(memory_space=pltpu.SMEM), pl.BlockSpec(memory_space=pltpu.VMEM)]
        + [hbm] * 4,
        out_specs=pl.BlockSpec(memory_space=pl.ANY),
        scratch_shapes=[
            pltpu.VMEM((4, 2, 512, 512), BF),
            pltpu.VMEM((4, 2, 512, 512), BF),
            pltpu.VMEM((8, 16, 2, 2048), BF),
            pltpu.VMEM((MATRICES, 256, 256), BF),
            pltpu.VMEM((512, 512), BF),
            pltpu.VMEM((4, 512, 1024), BF),
            pltpu.VMEM((8, 512, 128), BF),
            pltpu.VMEM((128, 32, 128), BF),
            pltpu.VMEM((128, 16, 128), BF),
            exchange,
            exchange,
            exchange,
            pltpu.VMEM((4, 2, 512, 128), BF),
            pltpu.VMEM((4, 512, 1024), F32),
            halves,
            halves,
            halves,
            pltpu.SemaphoreType.DMA((12,)),
            pltpu.SemaphoreType.DMA((CHUNKS,)),
            pltpu.SemaphoreType.DMA((CHUNKS,)),
            pltpu.SemaphoreType.DMA((CHUNKS,)),
            pltpu.SemaphoreType.DMA((CHUNKS,)),
            pltpu.SemaphoreType.DMA((8,)),
            pltpu.SemaphoreType.DMA((4,)),
        ],
        compiler_params=pltpu.CompilerParams(
            collective_id=0, has_side_effects=True, vmem_limit_bytes=47 << 20
        ),
    )(
        block_of_slot,
        block_of_slot.reshape(1, 128),
        green_ret.reshape(4, 2, 512, 512),
        sigma_in.reshape(4, 2, 512, 512),
        screened.reshape(32, 16, 2, 2048),
        matrices(),
    )
    return result.reshape(2, 2, 2, 512, 512)


def solution(mesh):
    in_specs = (
        P("energy", "momentum", None, None, None),
        P("energy", "momentum", None, None, None),
        P(("energy", "momentum"), None, None, None, None),
        P(),
    )
    out_specs = P("energy", "momentum", None, None, None)
    return jax.shard_map(local, mesh=mesh, in_specs=in_specs, out_specs=out_specs, check_vma=False)
```

```python
import jax
import jax.numpy as jnp
import numpy as np
from jax import lax
from jax.experimental import pallas as pl
from jax.experimental.pallas import tpu as pltpu
from jax.sharding import PartitionSpec as P

BF = jnp.bfloat16
F32 = jnp.float32
CHUNKS = 4
WIDE = 128


def transforms():
    m, n = np.arange(16), np.arange(8)
    e, k = np.arange(16), np.arange(8)
    out = np.zeros((4, 256, 256), np.float64)
    for a in range(2):
        for b in range(2):
            steps = ((2 * m + a)[:, None, None, None] * e[None, None, :, None]) * 1.0 / 32
            steps = steps + ((2 * n + b)[None, :, None, None] * k[None, None, None, :]) * 1.0 / 16
            cos, sin = np.cos(2 * np.pi * steps), np.sin(2 * np.pi * steps)
            cols = np.zeros((2, 16, 8, 16, 8, 2))
            cols[0, ..., 0], cols[0, ..., 1] = cos, sin
            cols[1, ..., 0], cols[1, ..., 1] = -sin, cos
            cols = cols.reshape(2, 16, 8, 8, 2, 4, 2, 2).transpose(0, 1, 2, 3, 5, 4, 6, 7)
            out[2 * a + b] = cols.reshape(256, 256)
    return out


def weaver():
    row = np.arange(256)
    taken = (row % 8) * 32 + row // 8
    return np.arange(256)[None, :] == taken[:, None]


def splitter():
    row = np.arange(256)
    kind, part, m, n = row // 64, row // 32 % 2, row // 8 % 4, row % 8
    taken = ((2 * m + kind // 2) * 16 + 2 * n + kind % 2) * 2 + part
    return np.arange(256)[None, :] == taken[:, None]


def half_weaver():
    row = np.arange(256)
    taken = (row % 4) * 64 + row // 4
    return np.arange(256)[None, :] == taken[:, None]


def joiner():
    row = np.arange(256)
    chunk, source, line, point, part = row // 128, row // 32 % 4, row // 8 % 4, row // 2 % 4, row % 2
    taken = point * 64 + source * 16 + line * 4 + chunk * 2 + part
    return np.arange(256)[None, :] == taken[:, None]


def parter():
    row = np.arange(256)
    taken = (row // 16 % 8) * 32 + (row // 4 % 4) * 8 + (row // 128) * 4 + row % 4
    return np.arange(256)[None, :] == taken[:, None]


FORTH, BACK, WEAVE, UNWEAVE, SPLIT, HALF_WEAVE, HALF_UNWEAVE, JOIN, PART = 0, 4, 8, 9, 10, 11, 12, 13, 14
MATRICES, ROOM = 15, 40


def matrices():
    forth = transforms()
    moves = [weaver(), weaver().T, splitter(), half_weaver(), half_weaver().T, joiner(), parter()]
    spare = np.zeros((ROOM - MATRICES, 256, 256))
    return jnp.asarray(np.concatenate([forth, forth.transpose(0, 2, 1) / 512, np.stack(moves), spare]), BF)


def dot(a, b):
    return jnp.dot(a, b, preferred_element_type=F32)


def dot_t(a, b):
    return lax.dot_general(a, b, (((1,), (1,)), ((), ())), preferred_element_type=F32)


def beside(a, b):
    return jnp.concatenate([a, b], axis=1)


def above(a, b):
    return jnp.concatenate([a, b], axis=0)


def kernel(
    order, order_row, green, sigma, screened, tables, out,
    g, s, raw, mv, cols, first, gbuf, woven, half_woven, stage, got1, got2, sig, acc,
    half_stage, half_got, last_got, load_sem, send1, recv1, send2, recv2, half_sem, out_sem,
):
    e = lax.axis_index("energy")
    m = lax.axis_index("momentum")
    me = e * 8 + m
    my_z, my_y, my_x, my_core = e // 4, (m // 4) * 2 + (e // 2) % 2, m % 4, e % 2
    ys = [(my_y + i) % 4 for i in range(4)]
    zs = [(my_z + i) % 4 for i in range(4)]
    near = []
    for y in range(4):
        for z in range(4):
            for core in range(2):
                to_core = my_core if core == 0 else 1 - my_core
                near.append((zs[z] * 4 + (ys[y] % 2) * 2 + to_core, (ys[y] // 2) * 4))

    def each_partner(act):
        def at_x(x, _):
            xs = [(my_x + x + i) % 4 for i in range(4)]
            for k in range(32):
                to = (near[k][0], near[k][1] + xs[(k // 8 + k // 2) % 4])
                if k == 0:
                    pl.when(x > 0)(lambda to=to: act(to))
                else:
                    act(to)
            return 0

        lax.fori_loop(0, 4, at_x, 0)

    def load_point(pt):
        return (
            pltpu.make_async_copy(green.at[pt], g.at[pt], load_sem.at[pt]),
            pltpu.make_async_copy(sigma.at[pt], s.at[pt], load_sem.at[4 + pt]),
        )

    late = pltpu.make_async_copy(tables.at[pl.ds(0, MATRICES)], mv, load_sem.at[8])
    for pt in range(4):
        for copy in load_point(pt):
            copy.start()
    late.start()

    barrier = pltpu.get_barrier_semaphore()
    each_partner(
        lambda to: pl.semaphore_signal(
            barrier, inc=1, device_id=to, device_id_type=pl.DeviceIdType.MESH
        )
    )

    def make_first(pt, _):
        for copy in load_point(pt):
            copy.wait()
        sr, si = s[pt, 0], s[pt, 1]
        first[pt] = dot(beside(g[pt, 0], g[pt, 1]), above(beside(sr, si), beside(-si, sr))).astype(BF)
        return 0

    def green_of(chunk):
        here = pl.ds(pl.multiple_of(chunk * WIDE, WIDE), WIDE)

        def make_green(pt, _):
            gr, gi = g[pt, 0, here, :], g[pt, 1, here, :]
            both = dot_t(first[pt], above(beside(gr, gi), beside(-gi, gr))).astype(BF)
            gbuf[2 * pt] = both[:, :WIDE]
            gbuf[2 * pt + 1] = both[:, WIDE:]
            return 0

        return make_green

    for pt in range(4):
        make_first(pt, 0)
        gr, gi = g[pt, 0, : 2 * WIDE, :], g[pt, 1, : 2 * WIDE, :]
        early = dot_t(first[pt], above(beside(gr, gi), beside(-gi, gr))).astype(BF)
        for chunk in range(2):
            for part in range(2):
                at = (2 * part + chunk) * WIDE
                gbuf[2 * chunk + part] = early[:, at : at + WIDE]
        if pt == 0:
            late.wait()

        def early_weave(group, _):
            both = [
                gbuf[0:4, pl.ds(pl.multiple_of((2 * group + h) * 64, 64), 64), :].reshape(256, 128)
                for h in range(2)
            ]
            mixed = dot(mv[HALF_WEAVE], beside(*both)).astype(BF)
            for h in range(2):
                piece = mixed[:, 128 * h : 128 * (h + 1)].reshape(16, 16, 128)
                half_woven[pl.ds((2 * group + h) * 16, 16)] = piece
            return 0

        lax.fori_loop(0, 4, early_weave, 0)
        if pt == 0:
            pl.semaphore_wait(barrier, 127)

        def send_early(to):
            slot = to[0] * 8 + to[1]
            half_stage[pt, slot] = half_woven[order[slot]]
            pltpu.make_async_remote_copy(
                half_stage.at[pt, slot],
                half_got.at[pt, me],
                half_sem.at[pt],
                half_sem.at[4 + pt],
                device_id=to,
                device_id_type=pl.DeviceIdType.MESH,
            ).start()

        each_partner(send_early)
        half_got[pt, me] = half_woven[order[me]]

    def outward(chunk, _):
        lax.fori_loop(0, 4, green_of(chunk), 0)

        def weave(group, _):
            both = [
                gbuf[:, pl.ds(pl.multiple_of((2 * group + h) * 32, 32), 32), :].reshape(256, 128)
                for h in range(2)
            ]
            mixed = dot(mv[WEAVE], beside(*both)).astype(BF)
            for h in range(2):
                piece = mixed[:, 128 * h : 128 * (h + 1)].reshape(8, 32, 128)
                woven[pl.ds((2 * group + h) * 8, 8)] = piece
            return 0

        lax.fori_loop(0, 8, weave, 0)

        def send(to):
            slot = to[0] * 8 + to[1]
            stage[chunk, slot] = woven[order[slot]]
            pltpu.make_async_remote_copy(
                stage.at[chunk, slot],
                got1.at[chunk, me],
                send1.at[chunk],
                recv1.at[chunk],
                device_id=to,
                device_id_type=pl.DeviceIdType.MESH,
            ).start()

        each_partner(send)
        got1[chunk, me] = woven[order[me]]
        return 0

    lax.fori_loop(2, CHUNKS, outward, 0)

    lane = lax.broadcasted_iota(jnp.int32, (128, 512), 1)
    slot = lax.broadcasted_iota(jnp.int32, (128, 512), 0)
    spread = (slot == lane // 4).astype(F32).astype(BF)
    blocks = jnp.broadcast_to(order_row[...].astype(F32), (8, 128)).astype(BF)
    lane1 = lax.broadcasted_iota(jnp.int32, (1, 512), 1)
    target = dot(blocks, spread)[0:1] * 4.0 + (lane1 % 4).astype(F32)
    index = lax.broadcasted_iota(jnp.int32, (512, 512), 0).astype(F32)
    cols[...] = jnp.where(index == target, 1.0, 0.0).astype(BF)

    def make_gcol(pt, _):
        for part in range(2):
            first[pt, :, 512 * part : 512 * part + 512] = dot(g[pt, part], cols[...]).astype(BF)
        return 0

    lax.fori_loop(0, 4, make_gcol, 0)

    def split(group, _):
        load = pltpu.make_async_copy(screened.at[pl.ds(group * 8, 8)], raw, load_sem.at[11])
        load.start()
        load.wait()
        parted = dot(mv[SPLIT], raw[...].reshape(256, 2048)).astype(BF)
        for row in range(4):
            at = pl.ds(pl.multiple_of(row * 128 + group * 32, 32), 32)
            s[:, :, at, :] = parted[:, 512 * row : 512 * row + 512].reshape(4, 2, 32, 512)
        return 0

    lax.fori_loop(0, 4, split, 0)

    some = pl.ds(0, 127)

    def whole(piece, sem):
        return pltpu.make_async_copy(
            half_stage.at[piece, some], half_got.at[piece, some], half_sem.at[sem + piece]
        )

    for pt in range(4):
        whole(pt, 4).wait()

    def join(group, _):
        both = [half_got[:, pl.ds((2 * group + h) * 4, 4)].reshape(256, 128) for h in range(2)]
        mixed = dot(mv[JOIN], beside(*both)).astype(BF)
        for h in range(2):
            piece = mixed[:, 128 * h : 128 * (h + 1)].reshape(2, 4, 32, 128)
            got1[0:2, pl.ds((2 * group + h) * 4, 4)] = piece
        return 0

    lax.fori_loop(0, 16, join, 0)
    for pt in range(4):
        whole(pt, 0).wait()

    def convolve(chunk, _):
        @pl.when(chunk > 1)
        def _():
            pltpu.make_async_copy(stage.at[chunk, some], got1.at[chunk, some], recv1.at[chunk]).wait()
            pltpu.make_async_copy(stage.at[chunk, some], got1.at[chunk, some], send1.at[chunk]).wait()

        here = pl.ds(pl.multiple_of(chunk * WIDE, WIDE), WIDE)
        for pair in range(2):
            held = got1[chunk, :, 16 * pair : 16 * pair + 16, :].astype(F32)
            held = held.reshape(2, 8, 2, 4, 16, 128)
            plus = held[0] + held[1]
            minus = held[0] - held[1]
            parts = (
                plus[:, 0] + plus[:, 1],
                plus[:, 0] - plus[:, 1],
                minus[:, 0] + minus[:, 1],
                minus[:, 0] - minus[:, 1],
            )
            done = []
            for kind in range(4):
                x = parts[kind]
                x = beside(x[:, :, 0:8].reshape(256, 128), x[:, :, 8:16].reshape(256, 128))
                y = dot(mv[FORTH + kind], x.astype(BF))
                spans = [pl.ds((2 * pair + h) * 128, 128) for h in range(2)]
                wr = beside(*[s[kind, 0, at, here] for at in spans]).astype(F32)
                wi = beside(*[s[kind, 1, at, here] for at in spans]).astype(F32)
                yr, yi = y[:128], y[128:]
                z = above(yr * wr - yi * wi, yr * wi + yi * wr).astype(BF)
                done.append(dot(mv[BACK + kind], z))
            up, down = done[0] + done[1], done[2] + done[3]
            cross_up, cross_down = done[0] - done[1], done[2] - done[3]
            results = ((up + down, cross_up + cross_down), (up - down, cross_up - cross_down))
            for eh in range(2):
                for mh in range(2):
                    x = results[eh][mh]
                    x = jnp.concatenate(
                        [x[:, :128].reshape(8, 4, 8, 128), x[:, 128:].reshape(8, 4, 8, 128)], axis=2
                    ).astype(BF)
                    for low in range(8):
                        at = (8 * eh + low) * 8 + 4 * mh
                        stage[chunk, at : at + 4, 16 * pair : 16 * pair + 16, :] = x[low]

        def send(to):
            pltpu.make_async_remote_copy(
                stage.at[chunk, to[0] * 8 + to[1]],
                got2.at[chunk, me],
                send2.at[chunk],
                recv2.at[chunk],
                device_id=to,
                device_id_type=pl.DeviceIdType.MESH,
            ).start()

        @pl.when(chunk < CHUNKS - 1)
        def _():
            each_partner(send)
            got2[chunk, me] = stage[chunk, me]

        return 0

    lax.fori_loop(0, CHUNKS, convolve, 0)

    def part(group, _):
        both = [
            stage[CHUNKS - 1, pl.ds((2 * group + h) * 8, 8)].reshape(256, 128) for h in range(2)
        ]
        mixed = dot(mv[PART], beside(*both)).astype(BF)
        for h in range(2):
            piece = mixed[:, 128 * h : 128 * (h + 1)].reshape(2, 8, 16, 128)
            half_stage[0:2, pl.ds((2 * group + h) * 8, 8)] = piece
        return 0

    lax.fori_loop(0, 8, part, 0)
    for half in range(2):

        def send_last(to):
            pltpu.make_async_remote_copy(
                half_stage.at[half, to[0] * 8 + to[1]],
                last_got.at[half, me],
                half_sem.at[8 + half],
                half_sem.at[10 + half],
                device_id=to,
                device_id_type=pl.DeviceIdType.MESH,
            ).start()

        each_partner(send_last)
        last_got[half, me] = half_stage[half, me]

    def inward(chunk):
        span = slice(WIDE * chunk, WIDE * chunk + WIDE)

        def at_point(pt, _):
            sr, si = sig[pt, 0], sig[pt, 1]
            mine = dot(first[pt], above(beside(sr, si), beside(-si, sr))).astype(BF)
            gr, gi = g[pt, 0, :, span], g[pt, 1, :, span]
            total = dot_t(mine, above(beside(gr, gi), beside(-gi, gr)))
            if chunk > 0:
                total = total + acc[pt]
            if chunk < CHUNKS - 1:
                acc[pt] = total
            else:
                total = total.astype(BF)
                s[pt, 0] = total[:, :512]
                s[pt, 1] = total[:, 512:]
                pltpu.make_async_copy(s.at[pt], out.at[pt], out_sem.at[pt]).start()
            return 0

        return at_point

    for chunk in range(CHUNKS - 1):
        pltpu.make_async_copy(stage.at[chunk, some], got2.at[chunk, some], recv2.at[chunk]).wait()

        def unweave(group, _):
            both = [got2[chunk, pl.ds((2 * group + h) * 8, 8)].reshape(256, 128) for h in range(2)]
            parted = dot(mv[UNWEAVE], beside(*both)).astype(BF)
            for h in range(2):
                at = pl.ds(pl.multiple_of((2 * group + h) * 32, 32), 32)
                piece = parted[:, 128 * h : 128 * (h + 1)].reshape(4, 2, 32, 128)
                sig[:, 0, at, :] = piece[:, 0]
                sig[:, 1, at, :] = piece[:, 1]
            return 0

        lax.fori_loop(0, 8, unweave, 0)
        lax.fori_loop(0, 4, inward(chunk), 0)

    for half in range(2):
        whole(half, 10).wait()

        def half_unweave(group, _):
            both = [
                last_got[half, pl.ds((2 * group + h) * 16, 16)].reshape(256, 128) for h in range(2)
            ]
            parted = dot(mv[HALF_UNWEAVE], beside(*both)).astype(BF)
            for h in range(2):
                at = pl.ds(pl.multiple_of((2 * group + h) * 64, 64), 64)
                piece = parted[:, 128 * h : 128 * (h + 1)].reshape(2, 2, 64, 128)
                sig[2 * half : 2 * half + 2, :, at, :] = piece
            return 0

        lax.fori_loop(0, 4, half_unweave, 0)
        lax.fori_loop(2 * half, 2 * half + 2, inward(CHUNKS - 1), 0)

    for chunk in range(CHUNKS - 1):
        pltpu.make_async_copy(stage.at[chunk, some], got2.at[chunk, some], send2.at[chunk]).wait()
    for half in range(2):
        whole(half, 8).wait()
    for pt in range(4):
        pltpu.make_async_copy(s.at[pt], out.at[pt], out_sem.at[pt]).wait()


def local(green_ret, sigma_in, screened, block_of_slot):
    hbm = pl.BlockSpec(memory_space=pltpu.HBM)
    exchange = pltpu.VMEM((CHUNKS, 128, 32, 128), BF)
    quarters = pltpu.VMEM((4, 128, 16, 128), BF)
    result = pl.pallas_call(
        kernel,
        out_shape=jax.ShapeDtypeStruct((4, 2, 512, 512), BF),
        in_specs=[pl.BlockSpec(memory_space=pltpu.SMEM), pl.BlockSpec(memory_space=pltpu.VMEM)]
        + [hbm] * 4,
        out_specs=pl.BlockSpec(memory_space=pl.ANY),
        scratch_shapes=[
            pltpu.VMEM((4, 2, 512, 512), BF),
            pltpu.VMEM((4, 2, 512, 512), BF),
            pltpu.VMEM((8, 16, 2, 2048), BF),
            pltpu.VMEM((MATRICES, 256, 256), BF),
            pltpu.VMEM((512, 512), BF),
            pltpu.VMEM((4, 512, 1024), BF),
            pltpu.VMEM((8, 512, 128), BF),
            pltpu.VMEM((128, 32, 128), BF),
            pltpu.VMEM((128, 16, 128), BF),
            exchange,
            exchange,
            exchange,
            pltpu.VMEM((4, 2, 512, 128), BF),
            pltpu.VMEM((4, 512, 1024), F32),
            quarters,
            quarters,
            pltpu.VMEM((2, 128, 16, 128), BF),
            pltpu.SemaphoreType.DMA((12,)),
            pltpu.SemaphoreType.DMA((CHUNKS,)),
            pltpu.SemaphoreType.DMA((CHUNKS,)),
            pltpu.SemaphoreType.DMA((CHUNKS,)),
            pltpu.SemaphoreType.DMA((CHUNKS,)),
            pltpu.SemaphoreType.DMA((12,)),
            pltpu.SemaphoreType.DMA((4,)),
        ],
        compiler_params=pltpu.CompilerParams(
            collective_id=0, has_side_effects=True, vmem_limit_bytes=48 << 20
        ),
    )(
        block_of_slot,
        block_of_slot.reshape(1, 128),
        green_ret.reshape(4, 2, 512, 512),
        sigma_in.reshape(4, 2, 512, 512),
        screened.reshape(32, 16, 2, 2048),
        matrices(),
    )
    return result.reshape(2, 2, 2, 512, 512)


def solution(mesh):
    in_specs = (
        P("energy", "momentum", None, None, None),
        P("energy", "momentum", None, None, None),
        P(("energy", "momentum"), None, None, None, None),
        P(),
    )
    out_specs = P("energy", "momentum", None, None, None)
    return jax.shard_map(local, mesh=mesh, in_specs=in_specs, out_specs=out_specs, check_vma=False)
```

```python
import jax
import jax.numpy as jnp
import numpy as np
from jax import lax
from jax.experimental import pallas as pl
from jax.experimental.pallas import tpu as pltpu
from jax.sharding import PartitionSpec as P

BF = jnp.bfloat16
F32 = jnp.float32
CHUNKS = 4
WIDE = 128


def transforms():
    m, n = np.arange(16), np.arange(8)
    e, k = np.arange(16), np.arange(8)
    out = np.zeros((4, 256, 256), np.float64)
    for a in range(2):
        for b in range(2):
            steps = ((2 * m + a)[:, None, None, None] * e[None, None, :, None]) * 1.0 / 32
            steps = steps + ((2 * n + b)[None, :, None, None] * k[None, None, None, :]) * 1.0 / 16
            cos, sin = np.cos(2 * np.pi * steps), np.sin(2 * np.pi * steps)
            cols = np.zeros((2, 16, 8, 16, 8, 2))
            cols[0, ..., 0], cols[0, ..., 1] = cos, sin
            cols[1, ..., 0], cols[1, ..., 1] = -sin, cos
            cols = cols.reshape(2, 16, 8, 8, 2, 4, 2, 2).transpose(0, 1, 2, 3, 5, 4, 6, 7)
            out[2 * a + b] = cols.reshape(256, 256)
    return out


def weaver():
    row = np.arange(256)
    taken = (row % 8) * 32 + row // 8
    return np.arange(256)[None, :] == taken[:, None]


def splitter():
    row = np.arange(256)
    kind, part, m, n = row // 64, row // 32 % 2, row // 8 % 4, row % 8
    taken = ((2 * m + kind // 2) * 16 + 2 * n + kind % 2) * 2 + part
    return np.arange(256)[None, :] == taken[:, None]


def half_weaver():
    row = np.arange(256)
    taken = (row % 4) * 64 + row // 4
    return np.arange(256)[None, :] == taken[:, None]


def joiner():
    row = np.arange(256)
    chunk, source, line, point, part = row // 128, row // 32 % 4, row // 8 % 4, row // 2 % 4, row % 2
    taken = point * 64 + source * 16 + line * 4 + chunk * 2 + part
    return np.arange(256)[None, :] == taken[:, None]


def parter():
    row = np.arange(256)
    taken = (row // 16 % 8) * 32 + (row // 4 % 4) * 8 + (row // 128) * 4 + row % 4
    return np.arange(256)[None, :] == taken[:, None]


HALF_WEAVE, FORTH, BACK, WEAVE, UNWEAVE, SPLIT, HALF_UNWEAVE, JOIN, PART = 0, 1, 5, 9, 10, 11, 12, 13, 14
MATRICES, ROOM = 15, 40


def matrices():
    forth = transforms()
    moves = [weaver(), weaver().T, splitter(), half_weaver().T, joiner(), parter()]
    spare = np.zeros((ROOM - MATRICES, 256, 256))
    return jnp.asarray(np.concatenate([half_weaver()[None], forth, forth.transpose(0, 2, 1) / 512, np.stack(moves), spare]), BF)


def dot(a, b):
    return jnp.dot(a, b, preferred_element_type=F32)


def dot_t(a, b):
    return lax.dot_general(a, b, (((1,), (1,)), ((), ())), preferred_element_type=F32)


def beside(a, b):
    return jnp.concatenate([a, b], axis=1)


def above(a, b):
    return jnp.concatenate([a, b], axis=0)


def kernel(
    order, order_row, green, sigma, screened, tables, out,
    g, s, raw, mv, cols, first, gbuf, woven, half_woven, stage, got1, got2, sig, acc,
    half_stage, half_got, last_got, load_sem, send1, recv1, send2, recv2, half_sem,
):
    e = lax.axis_index("energy")
    m = lax.axis_index("momentum")
    me = e * 8 + m
    my_z, my_y, my_x, my_core = e // 4, (m // 4) * 2 + (e // 2) % 2, m % 4, e % 2
    ys = [(my_y + i) % 4 for i in range(4)]
    zs = [(my_z + i) % 4 for i in range(4)]
    near = []
    for y in range(4):
        for z in range(4):
            for core in range(2):
                to_core = my_core if core == 0 else 1 - my_core
                near.append((zs[z] * 4 + (ys[y] % 2) * 2 + to_core, (ys[y] // 2) * 4))

    def each_partner(act):
        def at_x(x, _):
            xs = [(my_x + x + i) % 4 for i in range(4)]
            for k in range(32):
                to = (near[k][0], near[k][1] + xs[(k // 8 + k // 2) % 4])
                if k == 0:
                    pl.when(x > 0)(lambda to=to: act(to))
                else:
                    act(to)
            return 0

        lax.fori_loop(0, 4, at_x, 0)

    def load_point(pt):
        return (
            pltpu.make_async_copy(green.at[pt], g.at[pt], load_sem.at[pt]),
            pltpu.make_async_copy(sigma.at[pt], s.at[pt], load_sem.at[4 + pt]),
        )

    soon = pltpu.make_async_copy(tables.at[0], mv.at[0], load_sem.at[9])
    rest = pl.ds(1, MATRICES - 1)
    late = pltpu.make_async_copy(tables.at[rest], mv.at[rest], load_sem.at[8])
    for pt in range(4):
        for copy in load_point(pt):
            copy.start()
        if pt == 0:
            soon.start()
    late.start()

    barrier = pltpu.get_barrier_semaphore()
    each_partner(
        lambda to: pl.semaphore_signal(
            barrier, inc=1, device_id=to, device_id_type=pl.DeviceIdType.MESH
        )
    )

    def make_first(pt, _):
        for copy in load_point(pt):
            copy.wait()
        sr, si = s[pt, 0], s[pt, 1]
        first[pt] = dot(beside(g[pt, 0], g[pt, 1]), above(beside(sr, si), beside(-si, sr))).astype(BF)
        return 0

    def green_of(chunk):
        here = pl.ds(pl.multiple_of(chunk * WIDE, WIDE), WIDE)

        def make_green(pt, _):
            gr, gi = g[pt, 0, here, :], g[pt, 1, here, :]
            both = dot_t(first[pt], above(beside(gr, gi), beside(-gi, gr))).astype(BF)
            gbuf[2 * pt] = both[:, :WIDE]
            gbuf[2 * pt + 1] = both[:, WIDE:]
            return 0

        return make_green

    for pt in range(4):
        make_first(pt, 0)
        gr, gi = g[pt, 0, : 2 * WIDE, :], g[pt, 1, : 2 * WIDE, :]
        early = dot_t(first[pt], above(beside(gr, gi), beside(-gi, gr))).astype(BF)
        for chunk in range(2):
            for part in range(2):
                at = (2 * part + chunk) * WIDE
                gbuf[2 * chunk + part] = early[:, at : at + WIDE]
        if pt == 0:
            soon.wait()

        def early_weave(group, _):
            both = [
                gbuf[0:4, pl.ds(pl.multiple_of((2 * group + h) * 64, 64), 64), :].reshape(256, 128)
                for h in range(2)
            ]
            mixed = dot(mv[HALF_WEAVE], beside(*both)).astype(BF)
            for h in range(2):
                piece = mixed[:, 128 * h : 128 * (h + 1)].reshape(16, 16, 128)
                half_woven[pl.ds((2 * group + h) * 16, 16)] = piece
            return 0

        lax.fori_loop(0, 4, early_weave, 0)
        if pt == 0:
            pl.semaphore_wait(barrier, 127)

        def send_early(to):
            slot = to[0] * 8 + to[1]
            half_stage[pt, slot] = half_woven[order[slot]]
            pltpu.make_async_remote_copy(
                half_stage.at[pt, slot],
                half_got.at[pt, me],
                half_sem.at[pt],
                half_sem.at[4 + pt],
                device_id=to,
                device_id_type=pl.DeviceIdType.MESH,
            ).start()

        each_partner(send_early)
        half_got[pt, me] = half_woven[order[me]]

    def outward(chunk, _):
        lax.fori_loop(0, 4, green_of(chunk), 0)

        def weave(group, _):
            both = [
                gbuf[:, pl.ds(pl.multiple_of((2 * group + h) * 32, 32), 32), :].reshape(256, 128)
                for h in range(2)
            ]
            mixed = dot(mv[WEAVE], beside(*both)).astype(BF)
            for h in range(2):
                piece = mixed[:, 128 * h : 128 * (h + 1)].reshape(8, 32, 128)
                woven[pl.ds((2 * group + h) * 8, 8)] = piece
            return 0

        lax.fori_loop(0, 8, weave, 0)

        def send(to):
            slot = to[0] * 8 + to[1]
            stage[chunk, slot] = woven[order[slot]]
            pltpu.make_async_remote_copy(
                stage.at[chunk, slot],
                got1.at[chunk, me],
                send1.at[chunk],
                recv1.at[chunk],
                device_id=to,
                device_id_type=pl.DeviceIdType.MESH,
            ).start()

        each_partner(send)
        got1[chunk, me] = woven[order[me]]
        return 0

    late.wait()
    lax.fori_loop(2, CHUNKS, outward, 0)

    lane = lax.broadcasted_iota(jnp.int32, (128, 512), 1)
    slot = lax.broadcasted_iota(jnp.int32, (128, 512), 0)
    spread = (slot == lane // 4).astype(F32).astype(BF)
    blocks = jnp.broadcast_to(order_row[...].astype(F32), (8, 128)).astype(BF)
    lane1 = lax.broadcasted_iota(jnp.int32, (1, 512), 1)
    target = dot(blocks, spread)[0:1] * 4.0 + (lane1 % 4).astype(F32)
    index = lax.broadcasted_iota(jnp.int32, (512, 512), 0).astype(F32)
    cols[...] = jnp.where(index == target, 1.0, 0.0).astype(BF)

    def make_gcol(pt, _):
        for part in range(2):
            first[pt, :, 512 * part : 512 * part + 512] = dot(g[pt, part], cols[...]).astype(BF)
        return 0

    lax.fori_loop(0, 4, make_gcol, 0)

    def split(group, _):
        load = pltpu.make_async_copy(screened.at[pl.ds(group * 8, 8)], raw, load_sem.at[11])
        load.start()
        load.wait()
        parted = dot(mv[SPLIT], raw[...].reshape(256, 2048)).astype(BF)
        for row in range(4):
            at = pl.ds(pl.multiple_of(row * 128 + group * 32, 32), 32)
            s[:, :, at, :] = parted[:, 512 * row : 512 * row + 512].reshape(4, 2, 32, 512)
        return 0

    lax.fori_loop(0, 4, split, 0)

    some = pl.ds(0, 127)

    def whole(piece, sem):
        return pltpu.make_async_copy(
            half_stage.at[piece, some], half_got.at[piece, some], half_sem.at[sem + piece]
        )

    for pt in range(4):
        whole(pt, 4).wait()

    def join(group, _):
        both = [half_got[:, pl.ds((2 * group + h) * 4, 4)].reshape(256, 128) for h in range(2)]
        mixed = dot(mv[JOIN], beside(*both)).astype(BF)
        for h in range(2):
            piece = mixed[:, 128 * h : 128 * (h + 1)].reshape(2, 4, 32, 128)
            got1[0:2, pl.ds((2 * group + h) * 4, 4)] = piece
        return 0

    lax.fori_loop(0, 16, join, 0)
    for pt in range(4):
        whole(pt, 0).wait()

    def convolve(chunk, _):
        @pl.when(chunk > 1)
        def _():
            pltpu.make_async_copy(stage.at[chunk, some], got1.at[chunk, some], recv1.at[chunk]).wait()
            pltpu.make_async_copy(stage.at[chunk, some], got1.at[chunk, some], send1.at[chunk]).wait()

        here = pl.ds(pl.multiple_of(chunk * WIDE, WIDE), WIDE)
        for pair in range(2):
            held = got1[chunk, :, 16 * pair : 16 * pair + 16, :].astype(F32)
            held = held.reshape(2, 8, 2, 4, 16, 128)
            plus = held[0] + held[1]
            minus = held[0] - held[1]
            parts = (
                plus[:, 0] + plus[:, 1],
                plus[:, 0] - plus[:, 1],
                minus[:, 0] + minus[:, 1],
                minus[:, 0] - minus[:, 1],
            )
            done = []
            for kind in range(4):
                x = parts[kind]
                x = beside(x[:, :, 0:8].reshape(256, 128), x[:, :, 8:16].reshape(256, 128))
                y = dot(mv[FORTH + kind], x.astype(BF))
                spans = [pl.ds((2 * pair + h) * 128, 128) for h in range(2)]
                wr = beside(*[s[kind, 0, at, here] for at in spans]).astype(F32)
                wi = beside(*[s[kind, 1, at, here] for at in spans]).astype(F32)
                yr, yi = y[:128], y[128:]
                z = above(yr * wr - yi * wi, yr * wi + yi * wr).astype(BF)
                done.append(dot(mv[BACK + kind], z))
            up, down = done[0] + done[1], done[2] + done[3]
            cross_up, cross_down = done[0] - done[1], done[2] - done[3]
            results = ((up + down, cross_up + cross_down), (up - down, cross_up - cross_down))
            for eh in range(2):
                for mh in range(2):
                    x = results[eh][mh]
                    x = jnp.concatenate(
                        [x[:, :128].reshape(8, 4, 8, 128), x[:, 128:].reshape(8, 4, 8, 128)], axis=2
                    ).astype(BF)
                    for low in range(8):
                        at = (8 * eh + low) * 8 + 4 * mh
                        stage[chunk, at : at + 4, 16 * pair : 16 * pair + 16, :] = x[low]

        def send(to):
            pltpu.make_async_remote_copy(
                stage.at[chunk, to[0] * 8 + to[1]],
                got2.at[chunk, me],
                send2.at[chunk],
                recv2.at[chunk],
                device_id=to,
                device_id_type=pl.DeviceIdType.MESH,
            ).start()

        @pl.when(chunk < CHUNKS - 1)
        def _():
            each_partner(send)
            got2[chunk, me] = stage[chunk, me]

        return 0

    lax.fori_loop(0, CHUNKS, convolve, 0)

    def part(group, _):
        both = [
            stage[CHUNKS - 1, pl.ds((2 * group + h) * 8, 8)].reshape(256, 128) for h in range(2)
        ]
        mixed = dot(mv[PART], beside(*both)).astype(BF)
        for h in range(2):
            piece = mixed[:, 128 * h : 128 * (h + 1)].reshape(2, 8, 16, 128)
            half_stage[0:2, pl.ds((2 * group + h) * 8, 8)] = piece
        return 0

    lax.fori_loop(0, 8, part, 0)
    for half in range(2):

        def send_last(to):
            pltpu.make_async_remote_copy(
                half_stage.at[half, to[0] * 8 + to[1]],
                last_got.at[half, me],
                half_sem.at[8 + half],
                half_sem.at[10 + half],
                device_id=to,
                device_id_type=pl.DeviceIdType.MESH,
            ).start()

        each_partner(send_last)
        last_got[half, me] = half_stage[half, me]

    def inward(chunk):
        span = slice(WIDE * chunk, WIDE * chunk + WIDE)

        def at_point(pt, _):
            sr, si = sig[pt, 0], sig[pt, 1]
            mine = dot(first[pt], above(beside(sr, si), beside(-si, sr))).astype(BF)
            gr, gi = g[pt, 0, :, span], g[pt, 1, :, span]
            total = dot_t(mine, above(beside(gr, gi), beside(-gi, gr)))
            if chunk > 0:
                total = total + acc[pt]
            if chunk < CHUNKS - 1:
                acc[pt] = total
            else:
                total = total.astype(BF)
                out[pt, 0] = total[:, :512]
                out[pt, 1] = total[:, 512:]
            return 0

        return at_point

    for chunk in range(CHUNKS - 1):
        pltpu.make_async_copy(stage.at[chunk, some], got2.at[chunk, some], recv2.at[chunk]).wait()

        def unweave(group, _):
            both = [got2[chunk, pl.ds((2 * group + h) * 8, 8)].reshape(256, 128) for h in range(2)]
            parted = dot(mv[UNWEAVE], beside(*both)).astype(BF)
            for h in range(2):
                at = pl.ds(pl.multiple_of((2 * group + h) * 32, 32), 32)
                piece = parted[:, 128 * h : 128 * (h + 1)].reshape(4, 2, 32, 128)
                sig[:, 0, at, :] = piece[:, 0]
                sig[:, 1, at, :] = piece[:, 1]
            return 0

        lax.fori_loop(0, 8, unweave, 0)
        lax.fori_loop(0, 4, inward(chunk), 0)

    for half in range(2):
        whole(half, 10).wait()

        def half_unweave(group, _):
            both = [
                last_got[half, pl.ds((2 * group + h) * 16, 16)].reshape(256, 128) for h in range(2)
            ]
            parted = dot(mv[HALF_UNWEAVE], beside(*both)).astype(BF)
            for h in range(2):
                at = pl.ds(pl.multiple_of((2 * group + h) * 64, 64), 64)
                piece = parted[:, 128 * h : 128 * (h + 1)].reshape(2, 2, 64, 128)
                sig[2 * half : 2 * half + 2, :, at, :] = piece
            return 0

        lax.fori_loop(0, 4, half_unweave, 0)
        lax.fori_loop(2 * half, 2 * half + 2, inward(CHUNKS - 1), 0)

    for chunk in range(CHUNKS - 1):
        pltpu.make_async_copy(stage.at[chunk, some], got2.at[chunk, some], send2.at[chunk]).wait()
    for half in range(2):
        whole(half, 8).wait()


def local(green_ret, sigma_in, screened, block_of_slot):
    hbm = pl.BlockSpec(memory_space=pltpu.HBM)
    exchange = pltpu.VMEM((CHUNKS, 128, 32, 128), BF)
    quarters = pltpu.VMEM((4, 128, 16, 128), BF)
    result = pl.pallas_call(
        kernel,
        out_shape=jax.ShapeDtypeStruct((4, 2, 512, 512), BF),
        in_specs=[pl.BlockSpec(memory_space=pltpu.SMEM), pl.BlockSpec(memory_space=pltpu.VMEM)]
        + [hbm] * 4,
        out_specs=pl.BlockSpec(memory_space=pltpu.VMEM),
        scratch_shapes=[
            pltpu.VMEM((4, 2, 512, 512), BF),
            pltpu.VMEM((4, 2, 512, 512), BF),
            pltpu.VMEM((8, 16, 2, 2048), BF),
            pltpu.VMEM((MATRICES, 256, 256), BF),
            pltpu.VMEM((512, 512), BF),
            pltpu.VMEM((4, 512, 1024), BF),
            pltpu.VMEM((8, 512, 128), BF),
            pltpu.VMEM((128, 32, 128), BF),
            pltpu.VMEM((128, 16, 128), BF),
            exchange,
            exchange,
            exchange,
            pltpu.VMEM((4, 2, 512, 128), BF),
            pltpu.VMEM((4, 512, 1024), F32),
            quarters,
            quarters,
            pltpu.VMEM((2, 128, 16, 128), BF),
            pltpu.SemaphoreType.DMA((12,)),
            pltpu.SemaphoreType.DMA((CHUNKS,)),
            pltpu.SemaphoreType.DMA((CHUNKS,)),
            pltpu.SemaphoreType.DMA((CHUNKS,)),
            pltpu.SemaphoreType.DMA((CHUNKS,)),
            pltpu.SemaphoreType.DMA((12,)),
        ],
        compiler_params=pltpu.CompilerParams(
            collective_id=0, has_side_effects=True, vmem_limit_bytes=48 << 20
        ),
    )(
        block_of_slot,
        block_of_slot.reshape(1, 128),
        green_ret.reshape(4, 2, 512, 512),
        sigma_in.reshape(4, 2, 512, 512),
        screened.reshape(32, 16, 2, 2048),
        matrices(),
    )
    return result.reshape(2, 2, 2, 512, 512)


def solution(mesh):
    in_specs = (
        P("energy", "momentum", None, None, None),
        P("energy", "momentum", None, None, None),
        P(("energy", "momentum"), None, None, None, None),
        P(),
    )
    out_specs = P("energy", "momentum", None, None, None)
    return jax.shard_map(local, mesh=mesh, in_specs=in_specs, out_specs=out_specs, check_vma=False)
```

```python
import jax
import jax.numpy as jnp
import numpy as np
from jax import lax
from jax.experimental import pallas as pl
from jax.experimental.pallas import tpu as pltpu
from jax.sharding import PartitionSpec as P

BF = jnp.bfloat16
F32 = jnp.float32
CHUNKS = 4
WIDE = 128


def transforms():
    m, n = np.arange(16), np.arange(8)
    e, k = np.arange(16), np.arange(8)
    out = np.zeros((4, 256, 256), np.float64)
    for a in range(2):
        for b in range(2):
            steps = ((2 * m + a)[:, None, None, None] * e[None, None, :, None]) * 1.0 / 32
            steps = steps + ((2 * n + b)[None, :, None, None] * k[None, None, None, :]) * 1.0 / 16
            cos, sin = np.cos(2 * np.pi * steps), np.sin(2 * np.pi * steps)
            cols = np.zeros((2, 16, 8, 16, 8, 2))
            cols[0, ..., 0], cols[0, ..., 1] = cos, sin
            cols[1, ..., 0], cols[1, ..., 1] = -sin, cos
            cols = cols.reshape(2, 16, 8, 8, 2, 4, 2, 2).transpose(0, 1, 2, 3, 5, 4, 6, 7)
            out[2 * a + b] = cols.reshape(256, 256)
    return out


def weaver():
    row = np.arange(256)
    taken = (row % 8) * 32 + row // 8
    return np.arange(256)[None, :] == taken[:, None]


def splitter():
    row = np.arange(256)
    kind, part, m, n = row // 64, row // 32 % 2, row // 8 % 4, row % 8
    taken = ((2 * m + kind // 2) * 16 + 2 * n + kind % 2) * 2 + part
    return np.arange(256)[None, :] == taken[:, None]


def half_weaver():
    row = np.arange(256)
    taken = (row % 4) * 64 + row // 4
    return np.arange(256)[None, :] == taken[:, None]


def joiner():
    row = np.arange(256)
    chunk, source, line, point, part = row // 128, row // 32 % 4, row // 8 % 4, row // 2 % 4, row % 2
    taken = point * 64 + source * 16 + line * 4 + chunk * 2 + part
    return np.arange(256)[None, :] == taken[:, None]


def parter():
    row = np.arange(256)
    taken = (row // 16 % 8) * 32 + (row // 4 % 4) * 8 + (row // 128) * 4 + row % 4
    return np.arange(256)[None, :] == taken[:, None]


HALF_WEAVE, FORTH, BACK, WEAVE, UNWEAVE, SPLIT, HALF_UNWEAVE, JOIN, PART = 0, 1, 5, 9, 10, 11, 12, 13, 14
MATRICES, ROOM = 15, 40


def matrices():
    forth = transforms()
    moves = [weaver(), weaver().T, splitter(), half_weaver().T, joiner(), parter()]
    spare = np.zeros((ROOM - MATRICES, 256, 256))
    return jnp.asarray(np.concatenate([half_weaver()[None], forth, forth.transpose(0, 2, 1) / 512, np.stack(moves), spare]), BF)


def dot(a, b):
    return jnp.dot(a, b, preferred_element_type=F32)


def dot_t(a, b):
    return lax.dot_general(a, b, (((1,), (1,)), ((), ())), preferred_element_type=F32)


def beside(a, b):
    return jnp.concatenate([a, b], axis=1)


def above(a, b):
    return jnp.concatenate([a, b], axis=0)


def kernel(
    order, order_row, green, sigma, screened, tables, out,
    g, s, raw, mv, cols, first, gbuf, woven, half_woven, stage, got1, got2, sig, acc,
    half_stage, half_got, last_got, load_sem, send1, recv1, send2, recv2, half_sem,
):
    e = lax.axis_index("energy")
    m = lax.axis_index("momentum")
    me = e * 8 + m
    my_z, my_y, my_x, my_core = e // 4, (m // 4) * 2 + (e // 2) % 2, m % 4, e % 2
    ys = [(my_y + i) % 4 for i in range(4)]
    zs = [(my_z + i) % 4 for i in range(4)]
    near = []
    for y in range(4):
        for z in range(4):
            for core in range(2):
                to_core = my_core if core == 0 else 1 - my_core
                near.append((zs[z] * 4 + (ys[y] % 2) * 2 + to_core, (ys[y] // 2) * 4))

    def each_partner(act):
        def at_x(x, _):
            xs = [(my_x + x + i) % 4 for i in range(4)]
            for k in range(32):
                to = (near[k][0], near[k][1] + xs[(k // 8 + k // 2) % 4])
                if k == 0:
                    pl.when(x > 0)(lambda to=to: act(to))
                else:
                    act(to)
            return 0

        lax.fori_loop(0, 4, at_x, 0)

    def load_point(pt):
        return (
            pltpu.make_async_copy(green.at[pt], g.at[pt], load_sem.at[pt]),
            pltpu.make_async_copy(sigma.at[pt], s.at[pt], load_sem.at[4 + pt]),
        )

    soon = pltpu.make_async_copy(tables.at[0], mv.at[0], load_sem.at[9])
    rest = pl.ds(1, MATRICES - 1)
    late = pltpu.make_async_copy(tables.at[rest], mv.at[rest], load_sem.at[8])
    for pt in range(4):
        for copy in load_point(pt):
            copy.start()
        if pt == 0:
            soon.start()
    late.start()

    barrier = pltpu.get_barrier_semaphore()
    each_partner(
        lambda to: pl.semaphore_signal(
            barrier, inc=1, device_id=to, device_id_type=pl.DeviceIdType.MESH
        )
    )

    def make_first(pt, _):
        for copy in load_point(pt):
            copy.wait()
        sr, si = s[pt, 0], s[pt, 1]
        first[pt] = dot(beside(g[pt, 0], g[pt, 1]), above(beside(sr, si), beside(-si, sr))).astype(BF)
        return 0

    def green_of(chunk):
        here = pl.ds(pl.multiple_of(chunk * WIDE, WIDE), WIDE)

        def make_green(pt, _):
            gr, gi = g[pt, 0, here, :], g[pt, 1, here, :]
            both = dot_t(first[pt], above(beside(gr, gi), beside(-gi, gr))).astype(BF)
            gbuf[2 * pt] = both[:, :WIDE]
            gbuf[2 * pt + 1] = both[:, WIDE:]
            return 0

        return make_green

    for pt in range(4):
        make_first(pt, 0)
        gr, gi = g[pt, 0, : 2 * WIDE, :], g[pt, 1, : 2 * WIDE, :]
        early = dot_t(first[pt], above(beside(gr, gi), beside(-gi, gr))).astype(BF)
        for chunk in range(2):
            for part in range(2):
                at = (2 * part + chunk) * WIDE
                gbuf[2 * chunk + part] = early[:, at : at + WIDE]
        if pt == 0:
            soon.wait()

        def early_weave(group, _):
            both = [
                gbuf[0:4, pl.ds(pl.multiple_of((2 * group + h) * 64, 64), 64), :].reshape(256, 128)
                for h in range(2)
            ]
            mixed = dot(mv[HALF_WEAVE], beside(*both)).astype(BF)
            for h in range(2):
                piece = mixed[:, 128 * h : 128 * (h + 1)].reshape(16, 16, 128)
                half_woven[pl.ds((2 * group + h) * 16, 16)] = piece
            return 0

        lax.fori_loop(0, 4, early_weave, 0)
        if pt == 0:
            pl.semaphore_wait(barrier, 127)

        def send_early(to):
            slot = to[0] * 8 + to[1]
            half_stage[pt, slot] = half_woven[order[slot]]
            pltpu.make_async_remote_copy(
                half_stage.at[pt, slot],
                half_got.at[pt, me],
                half_sem.at[pt],
                half_sem.at[4 + pt],
                device_id=to,
                device_id_type=pl.DeviceIdType.MESH,
            ).start()

        each_partner(send_early)
        half_got[pt, me] = half_woven[order[me]]

    def outward(chunk, _):
        lax.fori_loop(0, 4, green_of(chunk), 0)

        def weave(group, _):
            both = [
                gbuf[:, pl.ds(pl.multiple_of((2 * group + h) * 32, 32), 32), :].reshape(256, 128)
                for h in range(2)
            ]
            mixed = dot(mv[WEAVE], beside(*both)).astype(BF)
            for h in range(2):
                piece = mixed[:, 128 * h : 128 * (h + 1)].reshape(8, 32, 128)
                woven[pl.ds((2 * group + h) * 8, 8)] = piece
            return 0

        lax.fori_loop(0, 8, weave, 0)

        def send(to):
            slot = to[0] * 8 + to[1]
            stage[chunk, slot] = woven[order[slot]]
            pltpu.make_async_remote_copy(
                stage.at[chunk, slot],
                got1.at[chunk, me],
                send1.at[chunk],
                recv1.at[chunk],
                device_id=to,
                device_id_type=pl.DeviceIdType.MESH,
            ).start()

        each_partner(send)
        got1[chunk, me] = woven[order[me]]
        return 0

    late.wait()
    lax.fori_loop(2, CHUNKS, outward, 0)

    lane = lax.broadcasted_iota(jnp.int32, (128, 512), 1)
    slot = lax.broadcasted_iota(jnp.int32, (128, 512), 0)
    spread = (slot == lane // 4).astype(F32).astype(BF)
    blocks = jnp.broadcast_to(order_row[...].astype(F32), (8, 128)).astype(BF)
    lane1 = lax.broadcasted_iota(jnp.int32, (1, 512), 1)
    target = dot(blocks, spread)[0:1] * 4.0 + (lane1 % 4).astype(F32)
    index = lax.broadcasted_iota(jnp.int32, (512, 512), 0).astype(F32)
    cols[...] = jnp.where(index == target, 1.0, 0.0).astype(BF)

    def make_gcol(pt, _):
        for part in range(2):
            first[pt, :, 512 * part : 512 * part + 512] = dot(g[pt, part], cols[...]).astype(BF)
        return 0

    lax.fori_loop(0, 4, make_gcol, 0)

    def split(group, _):
        load = pltpu.make_async_copy(screened.at[pl.ds(group * 8, 8)], raw, load_sem.at[11])
        load.start()
        load.wait()
        parted = dot(mv[SPLIT], raw[...].reshape(256, 2048)).astype(BF)
        for row in range(4):
            at = pl.ds(pl.multiple_of(row * 128 + group * 32, 32), 32)
            s[:, :, at, :] = parted[:, 512 * row : 512 * row + 512].reshape(4, 2, 32, 512)
        return 0

    lax.fori_loop(0, 4, split, 0)

    some = pl.ds(0, 127)

    def whole(piece, sem):
        return pltpu.make_async_copy(
            half_stage.at[piece, some], half_got.at[piece, some], half_sem.at[sem + piece]
        )

    for pt in range(4):
        whole(pt, 4).wait()

    def join(group, _):
        both = [half_got[:, pl.ds((2 * group + h) * 4, 4)].reshape(256, 128) for h in range(2)]
        mixed = dot(mv[JOIN], beside(*both)).astype(BF)
        for h in range(2):
            piece = mixed[:, 128 * h : 128 * (h + 1)].reshape(2, 4, 32, 128)
            got1[0:2, pl.ds((2 * group + h) * 4, 4)] = piece
        return 0

    lax.fori_loop(0, 16, join, 0)
    for pt in range(4):
        whole(pt, 0).wait()

    def convolve(chunk, _):
        @pl.when(chunk > 1)
        def _():
            pltpu.make_async_copy(stage.at[chunk, some], got1.at[chunk, some], recv1.at[chunk]).wait()
            pltpu.make_async_copy(stage.at[chunk, some], got1.at[chunk, some], send1.at[chunk]).wait()

        here = pl.ds(pl.multiple_of(chunk * WIDE, WIDE), WIDE)
        for pair in range(2):
            held = got1[chunk, :, 16 * pair : 16 * pair + 16, :].astype(F32)
            held = held.reshape(2, 8, 2, 4, 16, 128)
            plus = held[0] + held[1]
            minus = held[0] - held[1]
            parts = (
                plus[:, 0] + plus[:, 1],
                plus[:, 0] - plus[:, 1],
                minus[:, 0] + minus[:, 1],
                minus[:, 0] - minus[:, 1],
            )
            done = []
            for kind in range(4):
                x = parts[kind]
                x = beside(x[:, :, 0:8].reshape(256, 128), x[:, :, 8:16].reshape(256, 128))
                y = dot(mv[FORTH + kind], x.astype(BF))
                spans = [pl.ds((2 * pair + h) * 128, 128) for h in range(2)]
                wr = beside(*[s[kind, 0, at, here] for at in spans]).astype(F32)
                wi = beside(*[s[kind, 1, at, here] for at in spans]).astype(F32)
                yr, yi = y[:128], y[128:]
                z = above(yr * wr - yi * wi, yr * wi + yi * wr).astype(BF)
                done.append(dot(mv[BACK + kind], z))
            up, down = done[0] + done[1], done[2] + done[3]
            cross_up, cross_down = done[0] - done[1], done[2] - done[3]
            results = ((up + down, cross_up + cross_down), (up - down, cross_up - cross_down))
            for eh in range(2):
                for mh in range(2):
                    x = results[eh][mh]
                    x = jnp.concatenate(
                        [x[:, :128].reshape(8, 4, 8, 128), x[:, 128:].reshape(8, 4, 8, 128)], axis=2
                    ).astype(BF)
                    for low in range(8):
                        at = (8 * eh + low) * 8 + 4 * mh
                        stage[chunk, at : at + 4, 16 * pair : 16 * pair + 16, :] = x[low]

        def send(to):
            pltpu.make_async_remote_copy(
                stage.at[chunk, to[0] * 8 + to[1]],
                got2.at[chunk, me],
                send2.at[chunk],
                recv2.at[chunk],
                device_id=to,
                device_id_type=pl.DeviceIdType.MESH,
            ).start()

        @pl.when(chunk < CHUNKS - 1)
        def _():
            each_partner(send)
            got2[chunk, me] = stage[chunk, me]

        return 0

    lax.fori_loop(0, CHUNKS, convolve, 0)

    def part(group, _):
        both = [
            stage[CHUNKS - 1, pl.ds((2 * group + h) * 8, 8)].reshape(256, 128) for h in range(2)
        ]
        mixed = dot(mv[PART], beside(*both)).astype(BF)
        for h in range(2):
            piece = mixed[:, 128 * h : 128 * (h + 1)].reshape(2, 8, 16, 128)
            half_stage[0:2, pl.ds((2 * group + h) * 8, 8)] = piece
        return 0

    lax.fori_loop(0, 8, part, 0)
    for half in range(2):

        def send_last(to):
            pltpu.make_async_remote_copy(
                half_stage.at[half, to[0] * 8 + to[1]],
                last_got.at[half, me],
                half_sem.at[8 + half],
                half_sem.at[10 + half],
                device_id=to,
                device_id_type=pl.DeviceIdType.MESH,
            ).start()

        each_partner(send_last)
        last_got[half, me] = half_stage[half, me]

    def inward(chunk):
        span = slice(WIDE * chunk, WIDE * chunk + WIDE)

        def at_point(pt, _):
            sr, si = sig[pt, 0], sig[pt, 1]
            mine = dot(first[pt], above(beside(sr, si), beside(-si, sr))).astype(BF)
            gr, gi = g[pt, 0, :, span], g[pt, 1, :, span]
            total = dot_t(mine, above(beside(gr, gi), beside(-gi, gr)))
            if chunk > 0:
                total = total + acc[pt]
            if chunk < CHUNKS - 1:
                acc[pt] = total
            else:
                total = total.astype(BF)
                out[pt, 0] = total[:, :512]
                out[pt, 1] = total[:, 512:]
            return 0

        return at_point

    for chunk in range(CHUNKS - 1):
        pltpu.make_async_copy(stage.at[chunk, some], got2.at[chunk, some], recv2.at[chunk]).wait()

        def unweave(group, _):
            both = [got2[chunk, pl.ds((2 * group + h) * 8, 8)].reshape(256, 128) for h in range(2)]
            parted = dot(mv[UNWEAVE], beside(*both)).astype(BF)
            for h in range(2):
                at = pl.ds(pl.multiple_of((2 * group + h) * 32, 32), 32)
                piece = parted[:, 128 * h : 128 * (h + 1)].reshape(4, 2, 32, 128)
                sig[:, 0, at, :] = piece[:, 0]
                sig[:, 1, at, :] = piece[:, 1]
            return 0

        lax.fori_loop(0, 8, unweave, 0)
        lax.fori_loop(0, 4, inward(chunk), 0)

    for half in range(2):
        whole(half, 10).wait()

        def half_unweave(group, _):
            both = [
                last_got[half, pl.ds((2 * group + h) * 16, 16)].reshape(256, 128) for h in range(2)
            ]
            parted = dot(mv[HALF_UNWEAVE], beside(*both)).astype(BF)
            for h in range(2):
                at = pl.ds(pl.multiple_of((2 * group + h) * 64, 64), 64)
                piece = parted[:, 128 * h : 128 * (h + 1)].reshape(2, 2, 64, 128)
                sig[2 * half : 2 * half + 2, :, at, :] = piece
            return 0

        lax.fori_loop(0, 4, half_unweave, 0)
        for pt in range(2 * half, 2 * half + 2):
            inward(CHUNKS - 1)(pt, 0)

    for chunk in range(CHUNKS - 1):
        pltpu.make_async_copy(stage.at[chunk, some], got2.at[chunk, some], send2.at[chunk]).wait()
    for half in range(2):
        whole(half, 8).wait()


def local(green_ret, sigma_in, screened, block_of_slot):
    hbm = pl.BlockSpec(memory_space=pltpu.HBM)
    exchange = pltpu.VMEM((CHUNKS, 128, 32, 128), BF)
    quarters = pltpu.VMEM((4, 128, 16, 128), BF)
    result = pl.pallas_call(
        kernel,
        out_shape=jax.ShapeDtypeStruct((4, 2, 512, 512), BF),
        in_specs=[pl.BlockSpec(memory_space=pltpu.SMEM), pl.BlockSpec(memory_space=pltpu.VMEM)]
        + [hbm] * 4,
        out_specs=pl.BlockSpec(memory_space=pltpu.VMEM),
        scratch_shapes=[
            pltpu.VMEM((4, 2, 512, 512), BF),
            pltpu.VMEM((4, 2, 512, 512), BF),
            pltpu.VMEM((8, 16, 2, 2048), BF),
            pltpu.VMEM((MATRICES, 256, 256), BF),
            pltpu.VMEM((512, 512), BF),
            pltpu.VMEM((4, 512, 1024), BF),
            pltpu.VMEM((8, 512, 128), BF),
            pltpu.VMEM((128, 32, 128), BF),
            pltpu.VMEM((128, 16, 128), BF),
            exchange,
            exchange,
            exchange,
            pltpu.VMEM((4, 2, 512, 128), BF),
            pltpu.VMEM((4, 512, 1024), F32),
            quarters,
            quarters,
            pltpu.VMEM((2, 128, 16, 128), BF),
            pltpu.SemaphoreType.DMA((12,)),
            pltpu.SemaphoreType.DMA((CHUNKS,)),
            pltpu.SemaphoreType.DMA((CHUNKS,)),
            pltpu.SemaphoreType.DMA((CHUNKS,)),
            pltpu.SemaphoreType.DMA((CHUNKS,)),
            pltpu.SemaphoreType.DMA((12,)),
        ],
        compiler_params=pltpu.CompilerParams(
            collective_id=0, has_side_effects=True, vmem_limit_bytes=48 << 20
        ),
    )(
        block_of_slot,
        block_of_slot.reshape(1, 128),
        green_ret.reshape(4, 2, 512, 512),
        sigma_in.reshape(4, 2, 512, 512),
        screened.reshape(32, 16, 2, 2048),
        matrices(),
    )
    return result.reshape(2, 2, 2, 512, 512)


def solution(mesh):
    in_specs = (
        P("energy", "momentum", None, None, None),
        P("energy", "momentum", None, None, None),
        P(("energy", "momentum"), None, None, None, None),
        P(),
    )
    out_specs = P("energy", "momentum", None, None, None)
    return jax.shard_map(local, mesh=mesh, in_specs=in_specs, out_specs=out_specs, check_vma=False)
```
